512 devices in a mesh: ctx: 16 (over x, y), exp: 32 (over z, core).
Axes of the slice: x: 4, y: 4, z: 16, core: 2. Of those that a mesh axis runs over, the one named last changes fastest.
Arguments:
- resid: bfloat16 [2048, 3072], P('ctx', 'exp'), may hold values from -37 to 37
- queries: bfloat16 [2048, 4096], P('ctx', 'exp'), may hold values from -6 to 6
- keys: bfloat16 [2048, 4096], P('ctx', 'exp'), may hold values from -0.01171875 to 0.01171875
- values: bfloat16 [2048, 4096], P('ctx', 'exp'), may hold values from -6 to 6
- log_decay: float32 [32, 2048], P('exp', 'ctx'), may hold values from -1.5 to 0
- w_out: bfloat16 [4096, 3072], P('exp'), may hold values from -0.1875 to 0.1875
- w_up: bfloat16 [32, 3072, 6144], P('exp', None, 'ctx'), may hold values from -0.07307089 to 0.07307089
- w_down: bfloat16 [32, 6144, 3072], P('exp', 'ctx'), may hold values from -0.076546554 to 0.076546554
- expert_ids: int32 [2048, 2], P('ctx'), may hold values from 0 to 31, all different within a row; in each aligned block of 128 rows (0 to 127, 128 to 255, ...) at most 16 rows name the same one
- route_weights: float32 [2048, 2], P('ctx'), may hold values from 0.3 to 1.5
- cotangent: bfloat16 [2048, 3072], P('ctx', 'exp'), may hold values from -6 to 6
Outputs:
- layer_out: bfloat16 [2048, 3072], P('ctx', 'exp')
- resid_grad: bfloat16 [2048, 3072], P('ctx', 'exp')
- q_grad: bfloat16 [2048, 4096], P('ctx', 'exp')
- k_grad: bfloat16 [2048, 4096], P('ctx', 'exp')
- v_grad: bfloat16 [2048, 4096], P('ctx', 'exp')
The draws below stay inside these ranges and needn't reach their ends.
Inputs may be any that keep to these rules, and one draw needn't show every extreme that they name: `expert_ids`: in each aligned block of 128 rows (the positions of one block) no expert is named by more than 16 rows; the two ids of a row differ.
All inputs are finite; a program needn't handle non-finite values.
Results may differ from the reference program's by a relative error of at most 0.02.
Values may be sent and summed in bfloat16 or wider, within the bound.
No kernel may reach another device: no remote copies, remote signals or barrier semaphores. Data moves between devices by JAX's collectives and lax.ppermute only.
A program may use at most 64 MiB of HBM per device.

```python
import math
import jax
import jax.numpy as jnp
import numpy as np
from jax import lax

D = 3072
DH = 128
HEAD_DEV = 1
ATTENTION_COUNT = 32
FF = 6144
FF_DEV = 384
EXPERTS = 32
TOP = 2
TOK_CTX = 128
TOKEN_SPAN = 2048
CAP = 16
N_CTX = 16
N_EXP = 32


def resid_parts(key):
    base_key = jax.random.fold_in(key, 11)
    sampler_seeds = jax.random.split(base_key, 3)
    base = jax.random.truncated_normal(sampler_seeds[0], -4.0, 4.0, (TOKEN_SPAN, D), jnp.float32)
    row_scale = jnp.exp(jax.random.uniform(sampler_seeds[1], (TOKEN_SPAN, 1), jnp.float32, math.log(0.3), math.log(3.0)))
    col_scale = jnp.exp(jax.random.uniform(sampler_seeds[2], (1, D), jnp.float32, math.log(0.3), math.log(3.0)))
    return (base, row_scale, col_scale)


def draw_resid(key, part):
    base, row_scale, col_scale = resid_parts(key)
    return (base * row_scale * col_scale).astype(jnp.bfloat16)


def draw_cotangent(key, part):
    base, row_scale, col_scale = resid_parts(key)
    noise_key = jax.random.fold_in(key, 41)
    noise = jax.random.truncated_normal(noise_key, -4.0, 4.0, (TOKEN_SPAN, D), jnp.float32)
    mixed = 0.6 * base * col_scale + 0.8 * noise
    return jnp.clip(mixed, -6.0, 6.0).astype(jnp.bfloat16)


def expert_common(key, index):
    shared_key = jax.random.fold_in(jax.random.fold_in(key, 31), index)
    return jax.random.truncated_normal(shared_key, -4.0, 4.0, (D, FF), jnp.float32)


def draw_w_up(key, part):

    def one_expert(index):
        return (expert_common(key, index) / math.sqrt(D)).astype(jnp.bfloat16)
    return lax.map(one_expert, jnp.arange(EXPERTS))


def draw_w_down(key, part):

    def one_expert(index):
        shared = expert_common(key, index).T
        own_key = jax.random.fold_in(jax.random.fold_in(key, 37), index)
        own = jax.random.truncated_normal(own_key, -4.0, 4.0, (FF, D), jnp.float32)
        return ((0.7 * shared + 0.71 * own) / math.sqrt(FF)).astype(jnp.bfloat16)
    return lax.map(one_expert, jnp.arange(EXPERTS))


def draw_log_decay(key, part):
    base_key = jax.random.fold_in(key, 23)
    sampler_seeds = jax.random.split(base_key, 6)
    fast = jax.random.randint(sampler_seeds[0], (ATTENTION_COUNT, 1), 0, 2) == 1
    fast_rate = jnp.exp(jax.random.uniform(sampler_seeds[1], (ATTENTION_COUNT, 1), jnp.float32, math.log(1.0 / 50.0), math.log(1.0 / 30.0)))
    slow_rate = jnp.exp(jax.random.uniform(sampler_seeds[2], (ATTENTION_COUNT, 1), jnp.float32, math.log(0.05), math.log(0.5))) / TOKEN_SPAN
    fading_speed = jnp.where(fast, fast_rate, slow_rate)
    noisy_perturbation = jax.random.uniform(sampler_seeds[3], (ATTENTION_COUNT, TOKEN_SPAN), jnp.float32, 0.5, 1.5)
    spike_offset = jax.random.randint(sampler_seeds[4], (ATTENTION_COUNT, 2), 0, TOKEN_SPAN)
    stacking_level = jax.random.uniform(sampler_seeds[5], (ATTENTION_COUNT, 2), jnp.float32, 0.22, 0.69)
    token_offset = jnp.arange(TOKEN_SPAN)[None, :]
    spike_clusters = jnp.where(token_offset == spike_offset[:, 0:1], stacking_level[:, 0:1], 0.0) + jnp.where(token_offset == spike_offset[:, 1:2], stacking_level[:, 1:2], 0.0)
    return -(fading_speed * noisy_perturbation + spike_clusters)


def with_spikes(result, stream_key, source, target, shards_of, factor):
    owner, partner = [(jnp.arange(result.shape[position]) // (result.shape[position] // shards_of)).reshape([-1 if axis == position else 1 for axis in range(result.ndim)]) for position in (source, target)]
    chosen = jax.random.permutation(stream_key, shards_of)[partner]
    strong = (owner == chosen) | (owner == (partner + shards_of // 2) % shards_of)
    return jnp.where(strong, factor * result, result)


def block_levels(stream_key, shape, cuts, least, high):
    factor_of, own = 1.0, jax.random.fold_in(stream_key, 6)
    for axis_at, shards_of in cuts:
        heights = jnp.exp(jax.random.uniform(jax.random.fold_in(own, axis_at), (shards_of,), jnp.float32, least / len(cuts), high / len(cuts)))
        factor_of = factor_of * jnp.repeat(heights, shape[axis_at] // shards_of).reshape([-1 if axis == axis_at else 1 for axis in range(len(shape))])
    return factor_of


def assign_block(rng, own, number, rows, number_of, top, reach, lean):
    ranking = jax.random.permutation(rng, number_of)
    heavy_load, common = shares(number_of, rows * top, reach, lean, True), shares(number_of, rows * top, reach, lean, False)
    places = jnp.arange(number_of)

    def named(sizes, turn):
        used = int((sizes > 0).sum())
        fixed = max(1, used // 4)
        passed = fixed + (places - fixed + turn * (used - fixed)) % max(1, number_of - fixed)
        return jnp.zeros((number_of,), jnp.int32).at[ranking[jnp.where(places < fixed, places, passed)]].set(jnp.asarray(sizes, jnp.int32))

    sizes = jnp.where(number % 4 == 0, named(heavy_load, number // 4), named(common, number - number // 4 - 1))
    mixed = jax.random.permutation(jax.random.fold_in(own, 3), number_of)
    giver, receiver = mixed[0:number_of // 2 * 2:2], mixed[1:number_of // 2 * 2:2]
    room = jnp.minimum(sizes[giver] - 1, reach - sizes[receiver]) // 2
    room = jnp.where((giver == ranking[0]) | (receiver == ranking[0]) | (sizes[receiver] == 0), 0, jnp.maximum(room, 0))
    passed = jax.random.randint(jax.random.fold_in(own, 4), (number_of // 2,), 0, 1 << 20) % (room + 1)
    sizes = sizes.at[giver].add(-passed).at[receiver].add(passed)
    items = jnp.searchsorted(jnp.cumsum(sizes), jnp.arange(rows * top), side="right").astype(jnp.int32)
    grid = items.reshape(top, rows).T
    grid = grid[jax.random.permutation(jax.random.fold_in(own, 1), rows)]
    turn = jax.random.randint(jax.random.fold_in(own, 2), (rows, 1), 0, top)
    return jnp.take_along_axis(grid, (jnp.arange(top)[None, :] + turn) % top, axis=1)


def shares(amount, total, reach, lean, full):
    weights = [(1 << 20) // math.isqrt(standing ** lean) + 1 for standing in range(1, amount + 1)]
    largest = reach if full else min(reach, max(-(-total // amount), total * weights[0] // sum(weights)))
    least = 1 if total - largest >= amount - 1 else 0
    given, surplus = [largest] + [least] * (amount - 1), total - largest - least * (amount - 1)
    while surplus > 0:
        movable = [i for i in range(1, amount) if given[i] < largest] or [i for i in range(1, amount) if given[i] < reach]
        pool, budget = sum([weights[i] for i in movable]), surplus
        for i in movable:
            addition = min(reach - given[i], max(1, budget * weights[i] // pool), surplus)
            given[i] = given[i] + addition
            surplus = surplus - addition
    return np.array(given)


def centred(key, extent, scale, bound, cuts=(), held_as=jnp.bfloat16):
    values = scale * jax.random.normal(key, extent, jnp.float32)
    if cuts:
        values = values * block_levels(key, extent, cuts, -0.22, 0.18)
    return jnp.clip(values, -bound, bound).astype(held_as)


def bell_draw_with(key, shape, spread, bound, shards, heavy, held_as=jnp.bfloat16):
    result = spread * jax.random.normal(key, shape, jnp.float32)
    if shards:
        result = result * block_levels(key, shape, shards, -0.22, 0.18)
    return jnp.clip(with_spikes(result, jax.random.fold_in(key, 3), *heavy), -bound, bound).astype(held_as)


def setup_inputs(seed: int = 0) -> dict:
    splits = jax.random.split(jax.random.key(seed), 12)
    resid = draw_resid(jax.random.fold_in(splits[11], 71), 0)
    queries = centred(splits[1], (TOKEN_SPAN, ATTENTION_COUNT * DH), 1.0, 6.0, ((0, 16), (1, 32)))
    keys = centred(splits[2], (TOKEN_SPAN, ATTENTION_COUNT * DH), (DH * TOKEN_SPAN) ** -0.5, 0.01171875, ((0, 16), (1, 32)))
    values = centred(splits[3], (TOKEN_SPAN, ATTENTION_COUNT * DH), 1.0, 6.0, ((0, 16), (1, 32)))
    log_decay = draw_log_decay(jax.random.fold_in(splits[11], 71), 0)
    w_out = bell_draw_with(splits[5], (ATTENTION_COUNT * DH, D), (ATTENTION_COUNT * DH) ** -0.5, 0.1875, ((0, 32),), (0, 1, 32, 2.75))
    w_up = draw_w_up(jax.random.fold_in(splits[11], 71), 0)
    w_down = draw_w_down(jax.random.fold_in(splits[11], 71), 0)
    expert_ids_keys = jax.random.split(jax.random.fold_in(splits[8], 1), TOKEN_SPAN // TOK_CTX)
    expert_ids_turns = jax.random.permutation(jax.random.fold_in(splits[8], 3), TOKEN_SPAN // TOK_CTX)
    expert_ids = jax.vmap(lambda own, number: assign_block(jax.random.fold_in(splits[8], 2), own, number, TOK_CTX, EXPERTS, TOP, CAP, 2))(expert_ids_keys, expert_ids_turns).reshape((TOKEN_SPAN, TOP))
    route_weights = jnp.clip(0.3 + 1.2 * jax.random.uniform(splits[9], (TOKEN_SPAN, TOP), jnp.float32) ** block_levels(splits[9], (TOKEN_SPAN, TOP), ((0, 16),), -0.2, 0.2), 0.3, 1.5)
    cotangent = draw_cotangent(jax.random.fold_in(splits[11], 71), 0)
    return {"resid": resid, "queries": queries, "keys": keys, "values": values, "log_decay": log_decay, "w_out": w_out, "w_up": w_up, "w_down": w_down, "expert_ids": expert_ids, "route_weights": route_weights, "cotangent": cotangent}


highest_score = lax.Precision.HIGHEST

def block_decays(decay_rows):
    cum = jnp.cumsum(decay_rows, axis=-1)
    last = cum[:, -1]
    token_offset = jnp.arange(decay_rows.shape[-1])
    causal = token_offset[:, None] >= token_offset[None, :]
    gaps = jnp.where(causal[None], cum[:, :, None] - cum[:, None, :], -jnp.inf)
    return (cum, last, jnp.exp(gaps))

def silu_grad(upper):
    sigma = jax.nn.sigmoid(upper)
    return sigma * (1.0 + upper * (1.0 - sigma))

def attention_forward(query_heads, head_keys, head_values, decay_heads):

    def advance(state, block):
        query_block, block_keys, block_values, decay_block = block
        cum, last, decay_matrix = block_decays(decay_block)
        router_scores = jnp.einsum('htd,hid->hti', query_block, block_keys, precision=highest_score)
        inner = jnp.einsum('hti,hid->htd', router_scores * decay_matrix, block_values, precision=highest_score)
        outer = jnp.exp(cum)[..., None] * jnp.einsum('htd,hde->hte', query_block, state, precision=highest_score)
        keep_mask = jnp.exp(last[:, None] - cum)[..., None]
        local = jnp.einsum('hid,hie->hde', block_keys * keep_mask, block_values, precision=highest_score)
        new_state = jnp.exp(last)[:, None, None] * state + local
        return (new_state, (inner + outer, state))
    start = jnp.zeros((ATTENTION_COUNT, DH, DH), jnp.float32)
    _, (outputs, incoming) = lax.scan(advance, start, (query_heads, head_keys, head_values, decay_heads))
    return (outputs, incoming)

def attention_backward(query_heads, head_keys, head_values, decay_heads, incoming, head_gradient):

    def retreat(carried_state, block):
        query_block, block_keys, block_values, decay_block, state_in, block_gradient = block
        cum, last, decay_matrix = block_decays(decay_block)
        keep_mask = jnp.exp(last[:, None] - cum)[..., None]
        router_scores = jnp.einsum('htd,hid->hti', query_block, block_keys, precision=highest_score) * decay_matrix
        score_gradient = jnp.einsum('coy,cwy->cow', block_gradient, block_values, precision=highest_score) * decay_matrix
        query_grad = jnp.einsum('hti,hia->hta', score_gradient, block_keys, precision=highest_score)
        query_grad = query_grad + jnp.exp(cum)[..., None] * jnp.einsum('htb,hab->hta', block_gradient, state_in, precision=highest_score)
        key_gradient = jnp.einsum('hti,hta->hia', score_gradient, query_block, precision=highest_score)
        key_gradient = key_gradient + keep_mask * jnp.einsum('qsv,qnv->qsn', block_values, carried_state, precision=highest_score)
        value_gradient = jnp.einsum('nyw,nyx->nwx', router_scores, block_gradient, precision=highest_score)
        value_gradient = value_gradient + keep_mask * jnp.einsum('sfc,scl->sfl', block_keys, carried_state, precision=highest_score)
        local = jnp.einsum('hta,htb->hab', query_block * jnp.exp(cum)[..., None], block_gradient, precision=highest_score)
        new_carried = local + jnp.exp(last)[:, None, None] * carried_state
        return (new_carried, (query_grad, key_gradient, value_gradient))
    start = jnp.zeros((ATTENTION_COUNT, DH, DH), jnp.float32)
    _, grads = lax.scan(retreat, start, (query_heads, head_keys, head_values, decay_heads, incoming, head_gradient), reverse=True)
    return grads

def to_heads(matrix):
    return matrix.astype(jnp.float32).reshape(N_CTX, TOK_CTX, ATTENTION_COUNT, DH).transpose(0, 2, 1, 3)

def from_heads(blocks):
    return blocks.transpose(0, 2, 1, 3).reshape(TOKEN_SPAN, ATTENTION_COUNT * DH).astype(jnp.bfloat16)

def route_slots(expert_ids):
    onehot = (expert_ids[:, :, None] == jnp.arange(EXPERTS)[None, None, :]).astype(jnp.int32)
    flat = onehot.reshape(N_CTX, TOK_CTX * TOP, EXPERTS)
    before = jnp.cumsum(flat, axis=1) - flat
    return lax.optimization_barrier(jnp.sum(before * flat, axis=2)).reshape(TOKEN_SPAN, TOP).astype(jnp.int32)

def reference(resid, queries, keys, values, log_decay, w_out, w_up, w_down, expert_ids, route_weights, cotangent):
    query_heads = to_heads(queries)
    head_keys = to_heads(keys)
    head_values = to_heads(values)
    decay_heads = log_decay.reshape(ATTENTION_COUNT, N_CTX, TOK_CTX).transpose(1, 0, 2)
    outputs, incoming = attention_forward(query_heads, head_keys, head_values, decay_heads)
    attn_heads = from_heads(outputs)
    head_groups = attn_heads.reshape(TOKEN_SPAN, N_EXP, HEAD_DEV * DH).transpose(1, 0, 2)
    weight_groups = w_out.reshape(N_EXP, HEAD_DEV * DH, D)

    def add_group(total, group):
        partial_sum = jnp.dot(group[0], group[1], preferred_element_type=jnp.float32).astype(jnp.bfloat16)
        partial_sum = lax.optimization_barrier(partial_sum)
        return (total + partial_sum.astype(jnp.float32), None)
    attn_sum, _ = lax.scan(add_group, jnp.zeros((TOKEN_SPAN, D), jnp.float32), (head_groups, weight_groups))
    attn = attn_sum.astype(jnp.bfloat16)
    residual = (resid.astype(jnp.float32) + attn.astype(jnp.float32)).astype(jnp.bfloat16)
    residual_f = residual.astype(jnp.float32)
    rstd = lax.rsqrt(lax.optimization_barrier(jnp.mean(residual_f * residual_f, axis=1)) + 1e-06)
    normed = (residual_f * rstd[:, None]).astype(jnp.bfloat16)
    slots = route_slots(expert_ids)
    block_of = (jnp.arange(TOKEN_SPAN) // TOK_CTX).astype(jnp.int32)
    block_idx = jnp.broadcast_to(block_of[:, None], (TOKEN_SPAN, TOP))
    expert_in = jnp.zeros((EXPERTS, N_CTX, CAP, D), jnp.bfloat16)
    expert_in = expert_in.at[expert_ids, block_idx, slots].set(jnp.broadcast_to(normed[:, None, :], (TOKEN_SPAN, TOP, D)))
    expert_in = expert_in.reshape(EXPERTS, N_CTX * CAP, D)

    def expert_forward(items):
        rows_in, up_weight, down_weight = items
        upper = jnp.dot(rows_in, up_weight, preferred_element_type=jnp.float32)
        act = jax.nn.silu(upper).astype(jnp.bfloat16)
        parts = jnp.einsum('rjf,jfd->rjd', act.reshape(N_CTX * CAP, N_CTX, FF_DEV).astype(jnp.float32), down_weight.reshape(N_CTX, FF_DEV, D).astype(jnp.float32))
        parts = lax.optimization_barrier(parts.astype(jnp.bfloat16))
        return lax.optimization_barrier(jnp.sum(parts.astype(jnp.float32), axis=1)).astype(jnp.bfloat16)
    expert_out = lax.map(expert_forward, (expert_in, w_up, w_down)).reshape(EXPERTS, N_CTX, CAP, D)
    routed = expert_out[expert_ids, block_idx, slots].astype(jnp.float32)
    layer_out = (residual_f + lax.optimization_barrier(jnp.sum(route_weights[:, :, None] * routed, axis=1))).astype(jnp.bfloat16)
    cot_f = cotangent.astype(jnp.float32)
    grad_in = jnp.zeros((EXPERTS, N_CTX, CAP, D), jnp.float32)
    grad_in = grad_in.at[expert_ids, block_idx, slots].set(route_weights[:, :, None] * cot_f[:, None, :])
    grad_in = grad_in.astype(jnp.bfloat16).reshape(EXPERTS, N_CTX * CAP, D)

    def expert_backward(items):
        rows_in, rows_grad, up_weight, down_weight = items
        upper = jnp.dot(rows_in, up_weight, preferred_element_type=jnp.float32)
        grad_act = jnp.dot(rows_grad, down_weight.T, preferred_element_type=jnp.float32)
        grad_up = (grad_act * silu_grad(upper)).astype(jnp.bfloat16)
        parts = jnp.einsum('rjf,djf->rjd', grad_up.reshape(N_CTX * CAP, N_CTX, FF_DEV).astype(jnp.float32), up_weight.reshape(D, N_CTX, FF_DEV).astype(jnp.float32))
        parts = lax.optimization_barrier(parts.astype(jnp.bfloat16))
        return lax.optimization_barrier(jnp.sum(parts.astype(jnp.float32), axis=1)).astype(jnp.bfloat16)
    grad_expert = lax.map(expert_backward, (expert_in, grad_in, w_up, w_down)).reshape(EXPERTS, N_CTX, CAP, D)
    grad_normed = lax.optimization_barrier(jnp.sum(grad_expert[expert_ids, block_idx, slots].astype(jnp.float32), axis=1))
    inner_dot = lax.optimization_barrier(jnp.sum(grad_normed * residual_f, axis=1))
    grad_resid = rstd[:, None] * grad_normed - residual_f * (rstd * rstd * rstd * inner_dot / D)[:, None]
    resid_grad = (cot_f + grad_resid).astype(jnp.bfloat16)
    grad_flat = jnp.dot(resid_grad, w_out.T, preferred_element_type=jnp.float32)
    head_gradient = grad_flat.reshape(N_CTX, TOK_CTX, ATTENTION_COUNT, DH).transpose(0, 2, 1, 3)
    query_grad, key_gradient, value_gradient = attention_backward(query_heads, head_keys, head_values, decay_heads, incoming, head_gradient)
    return (layer_out, resid_grad, from_heads(query_grad), from_heads(key_gradient), from_heads(value_gradient))
```

```python
import jax
import jax.numpy as jnp
from jax import lax
from jax.sharding import PartitionSpec as P

highest = lax.Precision.HIGHEST
bf16 = jnp.bfloat16
f32 = jnp.float32


def mm(a, b, dims):
    return lax.dot_general(a, b, (dims, ((), ())), preferred_element_type=f32)


def mm_high(a, b, dims):
    return lax.dot_general(a, b, (dims, ((), ())), precision=highest, preferred_element_type=f32)


def gather_ctx(block):
    count = lax.axis_size("ctx")
    copies = jnp.broadcast_to(block[None], (count, *block.shape))
    return lax.all_to_all(copies, "ctx", 0, 0)


def between(lasts, low, high):
    count = lasts.shape[0]
    block = jnp.arange(count)
    inside = (block[None, :] > low) & (block[None, :] < high)
    return jnp.exp(jnp.sum(jnp.where(inside, lasts[None, :], 0.0), axis=1))


def local(
    resid, queries, keys, values, log_decay, w_out, w_up, w_down, expert_ids, route_weights, cotangent
):
    n_ctx, n_exp = lax.axis_size("ctx"), lax.axis_size("exp")
    chips = n_exp // 2
    me_ctx, me_exp = lax.axis_index("ctx"), lax.axis_index("exp")
    core = lax.rem(me_exp, 2)
    tokens, dh = queries.shape
    width = w_out.shape[1]
    share = width // n_exp
    cap = 4 * tokens // n_exp
    partner = [(i, i ^ 1) for i in range(n_exp)]
    same_core = [[2 * z + c for z in range(chips)] for c in range(2)]

    q, k, v = queries.astype(f32), keys.astype(f32), values.astype(f32)
    at = jnp.arange(tokens)
    causal = at[:, None] >= at[None, :]
    cum = jnp.sum(jnp.where(causal, log_decay, 0.0), axis=1)
    last = cum[-1]
    decay = jnp.exp(jnp.where(causal, cum[:, None] - cum[None, :], -jnp.inf))
    grow = jnp.exp(cum)[:, None]
    keep = jnp.exp(last - cum)[:, None]
    scores = mm_high(q, k, ((1,), (1,))) * decay
    state = mm_high(k * keep, v, ((0,), (0,)))
    high = lax.reduce_precision(last, 8, 7)
    mid = lax.reduce_precision(last - high, 8, 7)
    low = last - high - mid
    row = jnp.arange(16)[:, None]
    tail = jnp.where(row == 0, high, jnp.where(row == 1, mid, jnp.where(row == 2, low, 0.0)))
    packed = jnp.concatenate([state, jnp.broadcast_to(tail, (16, dh))], axis=0).astype(bf16)
    arrived = gather_ctx(packed).astype(f32)
    lasts = jnp.sum(arrived[:, dh : dh + 3, 0], axis=1)
    blocks = jnp.arange(n_ctx)
    weight_in = jnp.where(blocks < me_ctx, between(lasts, blocks[:, None], me_ctx), 0.0)
    incoming = jnp.sum(weight_in[:, None, None] * arrived[:, :dh], axis=0)
    attn_heads = (
        mm_high(scores, v, ((1,), (0,))) + grow * mm_high(q, incoming, ((1,), (0,)))
    ).astype(bf16)

    w_parts = w_out.T.reshape(chips, 2, share, dh).transpose(1, 0, 2, 3)
    partial = mm(w_parts.reshape(width, dh), attn_heads, ((1,), (1,))).astype(bf16)
    partial = partial.reshape(2, chips, share, tokens)
    mine = lax.dynamic_index_in_dim(partial, core, 0, False)
    other = lax.dynamic_index_in_dim(partial, 1 - core, 0, False)
    other = lax.ppermute(other, "exp", partner)
    pair = (mine.astype(f32) + other.astype(f32)).astype(bf16)
    pieces = lax.all_to_all(pair, "exp", 0, 0, axis_index_groups=same_core)
    attn = jnp.sum(pieces.astype(f32), axis=0).T.astype(bf16)
    residual = (resid.astype(f32) + attn.astype(f32)).astype(bf16)

    chosen = (expert_ids[:, :, None] == jnp.arange(n_exp)[None, None, :]).astype(f32)
    earlier = (at[:, None] > at[None, :]).astype(bf16)
    before = mm(earlier, jnp.sum(chosen, axis=1).astype(bf16), ((1,), (0,)))
    slots = jnp.sum(before[:, None, :] * chosen, axis=2).astype(jnp.int32)
    position = expert_ids * cap + slots
    picks = jnp.concatenate(
        [
            (position[:, j][:, None] == jnp.arange(n_exp * cap)[None, :]).astype(bf16)
            for j in range(2)
        ],
        axis=0,
    )
    cot = cotangent.astype(f32)
    parts = jnp.concatenate(
        [
            jnp.concatenate([residual, (route_weights[:, j : j + 1] * cot).astype(bf16)], axis=1)
            for j in range(2)
        ],
        axis=0,
    )
    sent = mm(picks, parts, ((0,), (0,))).astype(bf16).reshape(n_exp, cap, 2 * share)
    rows = lax.all_to_all(sent, "exp", 0, 0)
    rows = rows.reshape(n_exp, cap, 2, share).transpose(2, 1, 0, 3).reshape(2, cap, width)
    rows_f = rows[0].astype(f32)
    rstd = lax.rsqrt(jnp.mean(rows_f * rows_f, axis=1, keepdims=True) + 1e-6)
    normed = (rows_f * rstd).astype(bf16)

    everyone = gather_ctx(jnp.concatenate([normed, rows[1]], axis=0))
    x = everyone[:, :cap].reshape(n_ctx * cap, width)
    g = everyone[:, cap:].reshape(n_ctx * cap, width)
    up_w, down_w = w_up[0], w_down[0]
    upper = mm(x, up_w, ((1,), (0,)))
    grad_act = mm(g, down_w, ((1,), (1,)))
    sigma = jax.nn.sigmoid(upper)
    act = (upper * sigma).astype(bf16)
    grad_up = (grad_act * (sigma * (1.0 + upper * (1.0 - sigma)))).astype(bf16)
    out = mm(act, down_w, ((1,), (0,))).astype(bf16).reshape(n_ctx, cap, width)
    back = mm(grad_up, up_w, ((1,), (1,))).astype(bf16).reshape(n_ctx, cap, width)
    sums = lax.all_to_all(jnp.concatenate([out, back], axis=1), "ctx", 0, 0)
    sums = jnp.sum(sums.astype(f32), axis=0)
    grad_rows = sums[cap:]
    inner = jnp.sum(grad_rows * rows_f, axis=1, keepdims=True)
    grad_rows = rstd * grad_rows - rows_f * (rstd * rstd * rstd * inner / width)
    both = jnp.stack([sums[:cap], grad_rows]).astype(bf16)
    both = both.reshape(2, cap, n_exp, share).transpose(2, 1, 0, 3).reshape(n_exp, cap, 2 * share)
    returned = lax.all_to_all(both, "exp", 0, 0).reshape(n_exp * cap, 2 * share)
    routed = mm(picks, returned, ((1,), (0,)))
    first, second = routed[:tokens], routed[tokens:]
    layer_out = (
        residual.astype(f32)
        + (route_weights[:, :1] * first[:, :share] + route_weights[:, 1:] * second[:, :share])
    ).astype(bf16)
    resid_grad = (cot + (first[:, share:] + second[:, share:])).astype(bf16)

    own_parts = lax.all_gather(resid_grad.T, "exp", axis_index_groups=same_core)
    own_parts = own_parts.reshape(chips * share, tokens)
    other_parts = lax.ppermute(own_parts, "exp", partner)
    w_halves = w_parts.reshape(2, chips * share, dh)
    w_mine = lax.dynamic_index_in_dim(w_halves, core, 0, False)
    w_other = lax.dynamic_index_in_dim(w_halves, 1 - core, 0, False)
    grad_heads = mm(own_parts, w_mine, ((0,), (0,))) + mm(other_parts, w_other, ((0,), (0,)))
    state_grad = mm_high(q * grow, grad_heads, ((0,), (0,)))
    arrived = gather_ctx(state_grad.astype(bf16)).astype(f32)
    weight_back = jnp.where(blocks > me_ctx, between(lasts, me_ctx, blocks[:, None]), 0.0)
    carried = jnp.sum(weight_back[:, None, None] * arrived, axis=0)
    score_grad = mm_high(grad_heads, v, ((1,), (1,))) * decay
    q_grad = mm_high(score_grad, k, ((1,), (0,)))
    q_grad = q_grad + grow * mm_high(grad_heads, incoming, ((1,), (1,)))
    k_grad = mm_high(score_grad, q, ((0,), (0,)))
    k_grad = k_grad + keep * mm_high(v, carried, ((1,), (1,)))
    v_grad = mm_high(scores, grad_heads, ((0,), (0,)))
    v_grad = v_grad + keep * mm_high(k, carried, ((1,), (0,)))
    return (layer_out, resid_grad, q_grad.astype(bf16), k_grad.astype(bf16), v_grad.astype(bf16))


def solution(mesh):
    both = P("ctx", "exp")
    rows = P("ctx", None)
    return jax.shard_map(
        local,
        mesh=mesh,
        in_specs=(
            both, both, both, both, P("exp", "ctx"), P("exp", None),
            P("exp", None, "ctx"), P("exp", "ctx", None), rows, rows, both,
        ),
        out_specs=(both,) * 5,
        check_vma=False,
    )
```

```python
import functools

import jax
import jax.numpy as jnp
from jax import lax
from jax.experimental import pallas as pl
from jax.experimental.pallas import tpu as pltpu
from jax.sharding import PartitionSpec as P

bf16 = jnp.bfloat16
f32 = jnp.float32
ROWS = 16


def mm(a, b, dims):
    return lax.dot_general(a, b, (dims, ((), ())), preferred_element_type=f32)


def mm_high(a, b, dims):
    return lax.dot_general(
        a, b, (dims, ((), ())), precision=lax.Precision.HIGHEST, preferred_element_type=f32
    )


def iota(shape, axis):
    return lax.broadcasted_iota(jnp.int32, shape, axis)


def turned(column):
    n = column.shape[0]
    return jnp.sum(jnp.where(iota((n, n), 0) == iota((n, n), 1), column, 0.0), axis=0, keepdims=True)


def run_kernel(body, outs, args, smem=0, flops=0, moved=0, limit=24):
    vmem = pl.BlockSpec(memory_space=pltpu.VMEM)
    specs = [pl.BlockSpec(memory_space=pltpu.SMEM)] * smem + [vmem] * (len(args) - smem)
    return pl.pallas_call(
        body,
        out_shape=[jax.ShapeDtypeStruct(shape, dtype) for shape, dtype in outs],
        in_specs=specs,
        out_specs=[vmem] * len(outs),
        compiler_params=pltpu.CompilerParams(vmem_limit_bytes=limit << 20),
        cost_estimate=pl.CostEstimate(flops=flops, bytes_accessed=moved, transcendentals=0),
    )(*args)


def running(decay_row):
    n = decay_row.shape[1]
    causal = iota((n, n), 0) >= iota((n, n), 1)
    return jnp.sum(jnp.where(causal, decay_row, 0.0), axis=1, keepdims=True)


def state_kernel(keys, values, log_decay, packed):
    cum = running(log_decay[...])
    n = cum.shape[0]
    last = cum[n - 1 :, :]
    kept = keys[...].astype(f32) * jnp.exp(last - cum)
    state = mm_high(kept, values[...].astype(f32), ((0,), (0,))).astype(bf16)
    dh = state.shape[1]
    high = last.astype(bf16).astype(f32)
    mid = (last - high).astype(bf16).astype(f32)
    low = last - high - mid
    row = iota((ROWS, dh), 0)
    tail = jnp.where(row == 0, high, jnp.where(row == 1, mid, jnp.where(row == 2, low, 0.0)))
    for block in range(packed.shape[0]):
        packed[block, :dh, :] = state
        packed[block, dh:, :] = tail.astype(bf16)


def inner_kernel(queries, keys, values, log_decay, w_out, scores, inner, decay, grow, keep, w_turned):
    cum = running(log_decay[...])
    n = cum.shape[0]
    causal = iota((n, n), 0) >= iota((n, n), 1)
    gaps = jnp.where(causal, cum - turned(cum), 0.0)
    fall = jnp.where(causal, jnp.exp(gaps), 0.0)
    pairs = mm_high(queries[...].astype(f32), keys[...].astype(f32), ((1,), (1,))) * fall
    scores[...] = pairs
    decay[...] = fall
    inner[...] = mm_high(pairs, values[...].astype(f32), ((1,), (0,)))
    grow[...] = jnp.broadcast_to(jnp.exp(cum), grow.shape)
    keep[...] = jnp.broadcast_to(jnp.exp(cum[n - 1 :, :] - cum), keep.shape)
    dh = w_out.shape[0]
    for start in range(0, w_out.shape[1], dh):
        w_turned[start : start + dh, :] = w_out[:, start : start + dh].astype(f32).T.astype(bf16)


def route_kernel(ids, weights, cotangent, picks, picks_turned, cot_parts, *, cap):
    tokens = ids.shape[0]
    slots_all = picks.shape[1]
    experts = slots_all // cap
    chosen = [(ids[:, j : j + 1] == iota((tokens, experts), 1)).astype(f32) for j in range(2)]
    earlier = (iota((tokens, tokens), 0) > iota((tokens, tokens), 1)).astype(f32).astype(bf16)
    before = mm(earlier, (chosen[0] + chosen[1]).astype(bf16), ((1,), (0,)))
    cot = cotangent[...].astype(f32)
    for j in range(2):
        slot = jnp.sum(before * chosen[j], axis=1, keepdims=True)
        position = ids[:, j : j + 1].astype(f32) * cap + slot
        at = slice(j * tokens, (j + 1) * tokens)
        along = iota((tokens, slots_all), 1).astype(f32)
        picks[at, :] = (position == along).astype(f32).astype(bf16)
        down = iota((slots_all, tokens), 0).astype(f32)
        picks_turned[:, at] = (turned(position) == down).astype(f32).astype(bf16)
        cot_parts[at, :] = (weights[:, j : j + 1] * cot).astype(bf16)


def heads_kernel(place, arrived, queries, inner, grow, w_turned, mine, other, incoming):
    me, core = place[0], place[1]
    blocks = arrived.shape[0]
    dh = queries.shape[1]
    total = jnp.zeros((dh, dh), f32)
    gap = jnp.zeros((1, dh), f32)
    for block in reversed(range(blocks)):
        weight = jnp.where(block < me, jnp.exp(gap), 0.0)
        total = total + weight * arrived[block, :dh, :].astype(f32)
        last = jnp.sum(arrived[block, dh:, :].astype(f32), axis=0, keepdims=True)
        gap = gap + jnp.where(block < me, last, 0.0)
    incoming[...] = total
    outer = mm_high(queries[...].astype(f32), total, ((1,), (0,)))
    heads = (inner[...] + grow[...] * outer).astype(bf16)
    chips, share, _ = mine.shape
    turned_heads = heads.astype(f32).T.astype(bf16)
    for chip in range(chips):
        start = 2 * chip * share
        both = mm(w_turned[start : start + 2 * share, :], turned_heads, ((1,), (0,))).astype(bf16)
        even, odd = both[:share], both[share:]

        @pl.when(core == 0)
        def _():
            mine[chip] = even
            other[chip] = odd

        @pl.when(core != 0)
        def _():
            mine[chip] = odd
            other[chip] = even


def send_kernel(pieces, resid, cot_parts, picks_turned, residual, sent):
    attn = jnp.sum(pieces[...].astype(f32), axis=0).T.astype(bf16).astype(f32)
    total = (resid[...].astype(f32) + attn).astype(bf16)
    residual[...] = total
    tokens = total.shape[0]
    experts, cap, _ = sent.shape
    share = total.shape[1]
    placed = picks_turned[...]
    rows = mm(placed[:, :tokens] + placed[:, tokens:], total, ((1,), (0,))).astype(bf16)
    grads = mm(placed, cot_parts[...], ((1,), (0,))).astype(bf16)
    sent[:, :, :share] = rows.reshape(experts, cap, share)
    sent[:, :, share : 2 * share] = grads.reshape(experts, cap, share)


def norm_kernel(rows, packed, own, rstd_out):
    experts, cap, _ = rows.shape
    share = packed.shape[2] // experts
    whole = jnp.concatenate([rows[e, :, :share].astype(f32) for e in range(experts)], axis=1)
    grads = jnp.concatenate(
        [rows[e, :, share : 2 * share].astype(f32) for e in range(experts)], axis=1
    ).astype(bf16)
    width = whole.shape[1]
    rstd = lax.rsqrt(jnp.sum(whole * whole, axis=1, keepdims=True) / width + 1e-6)
    own[...] = whole.astype(bf16)
    rstd_out[...] = jnp.broadcast_to(rstd, rstd_out.shape)
    normed = (whole * rstd).astype(bf16)
    for block in range(packed.shape[0]):
        packed[block, :cap, :] = normed
        packed[block, cap:, :] = grads


def expert_kernel(everyone, w_up, w_down, sums, *, step):
    blocks, both, width = everyone.shape
    cap = both // 2
    rows = blocks * cap
    hidden = w_up.shape[1]

    def forward(i, carry):
        upper, grad_act = carry
        at = pl.ds(pl.multiple_of(i * step, step), step)
        x = everyone[:, :cap, at].reshape(rows, step)
        g = everyone[:, cap:, at].reshape(rows, step)
        upper = upper + mm(x, w_up[at, :], ((1,), (0,)))
        grad_act = grad_act + mm(g, w_down[:, at], ((1,), (1,)))
        return upper, grad_act

    zero = jnp.zeros((rows, hidden), f32)
    upper, grad_act = lax.fori_loop(0, width // step, forward, (zero, zero))
    sigma = 1.0 / (1.0 + jnp.exp(-upper))
    act = (upper * sigma).astype(bf16)
    grad_up = (grad_act * (sigma * (1.0 + upper * (1.0 - sigma)))).astype(bf16)

    def backward(i, carry):
        at = pl.ds(pl.multiple_of(i * step, step), step)
        out = mm(act, w_down[:, at], ((1,), (0,))).astype(bf16)
        back = mm(grad_up, w_up[at, :], ((1,), (1,))).astype(bf16)
        sums[:, :cap, at] = out.reshape(blocks, cap, step)
        sums[:, cap:, at] = back.reshape(blocks, cap, step)
        return carry

    lax.fori_loop(0, width // step, backward, 0)


def back_kernel(sums, own, rstd_in, returned):
    experts, cap, _ = returned.shape
    total = jnp.sum(sums[...].astype(f32), axis=0)
    out, grads = total[:cap], total[cap:]
    width = out.shape[1]
    share = width // experts
    rows = own[...].astype(f32)
    rstd = rstd_in[:, :1]
    grads = grads.astype(bf16).astype(f32)
    inner = jnp.sum(grads * rows, axis=1, keepdims=True)
    grads = rstd * grads - rows * (rstd * rstd * rstd * inner / width)
    for e in range(experts):
        at = slice(e * share, (e + 1) * share)
        returned[e, :, :share] = out[:, at].astype(bf16)
        returned[e, :, share : 2 * share] = grads[:, at].astype(bf16)


def join_kernel(returned, picks, weights, residual, cotangent, layer_out, resid_grad, turned_grad):
    tokens, share = residual.shape
    slots_all = picks.shape[1]
    rows = returned[...].reshape(slots_all, returned.shape[2])
    first = mm(picks[:tokens, :], rows, ((1,), (0,)))
    second = mm(picks[tokens:, :], rows, ((1,), (0,)))
    routed = weights[:, :1] * first[:, :share] + weights[:, 1:] * second[:, :share]
    layer_out[...] = (residual[...].astype(f32) + routed).astype(bf16)
    summed = first[:, share : 2 * share] + second[:, share : 2 * share]
    grad = (cotangent[...].astype(f32) + summed).astype(bf16)
    resid_grad[...] = grad
    turned_grad[...] = grad.astype(f32).T.astype(bf16)


def state_grad_kernel(turned_grads, w_out, queries, grow, grad_heads, packed):
    flipped = mm(w_out[...], turned_grads[...], ((1,), (0,)))
    grads = flipped.T
    grad_heads[...] = grads
    state = mm_high(queries[...].astype(f32) * grow[...], grads, ((0,), (0,))).astype(bf16)
    for block in range(packed.shape[0]):
        packed[block] = state


def grads_kernel(
    grad_heads, queries, keys, values, scores, decay, grow, incoming, q_grad, k_part, v_part
):
    grads = grad_heads[...]
    score_grad = mm_high(grads, values[...].astype(f32), ((1,), (1,))) * decay[...]
    direct = mm_high(score_grad, keys[...].astype(f32), ((1,), (0,)))
    carried = mm_high(grads, incoming[...], ((1,), (1,)))
    q_grad[...] = (direct + grow[...] * carried).astype(bf16)
    k_part[...] = mm_high(score_grad, queries[...].astype(f32), ((0,), (0,)))
    v_part[...] = mm_high(scores[...], grads, ((0,), (0,)))


def last_kernel(place, arrived, tails, keys, values, keep, k_part, v_part, k_grad, v_grad):
    me = place[0]
    blocks, dh, _ = arrived.shape
    total = jnp.zeros((dh, dh), f32)
    gap = jnp.zeros((1, dh), f32)
    for block in range(blocks):
        weight = jnp.where(block > me, jnp.exp(gap), 0.0)
        total = total + weight * arrived[block].astype(f32)
        last = jnp.sum(tails[block, dh:, :].astype(f32), axis=0, keepdims=True)
        gap = gap + jnp.where(block > me, last, 0.0)
    from_values = mm_high(values[...].astype(f32), total, ((1,), (1,)))
    from_keys = mm_high(keys[...].astype(f32), total, ((1,), (0,)))
    k_grad[...] = (k_part[...] + keep[...] * from_values).astype(bf16)
    v_grad[...] = (v_part[...] + keep[...] * from_keys).astype(bf16)


def local(
    resid, queries, keys, values, log_decay, w_out, w_up, w_down, expert_ids, route_weights, cotangent
):
    n_ctx, n_exp = lax.axis_size("ctx"), lax.axis_size("exp")
    chips = n_exp // 2
    place = jnp.stack([lax.axis_index("ctx"), lax.rem(lax.axis_index("exp"), 2)]).astype(jnp.int32)
    tokens, dh = queries.shape
    width = w_out.shape[1]
    share = width // n_exp
    cap = 4 * tokens // n_exp
    partner = [(i, i ^ 1) for i in range(n_exp)]
    same_core = [[2 * z + c for z in range(chips)] for c in range(2)]
    square = (tokens, dh)
    small = dict(flops=10_000_000, moved=1_000_000)

    [packed] = run_kernel(
        state_kernel, [((n_ctx, dh + ROWS, dh), bf16)], (keys, values, log_decay), **small
    )
    arrived = lax.all_to_all(packed, "ctx", 0, 0)
    scores, inner, decay, grow, keep, w_turned = run_kernel(
        inner_kernel,
        [((tokens, tokens), f32), (square, f32), ((tokens, tokens), f32), (square, f32), (square, f32)]
        + [((width, dh), bf16)],
        (queries, keys, values, log_decay, w_out),
        **small,
    )
    picks, picks_turned, cot_parts = run_kernel(
        functools.partial(route_kernel, cap=cap),
        [((2 * tokens, n_exp * cap), bf16), ((n_exp * cap, 2 * tokens), bf16)]
        + [((2 * tokens, share), bf16)],
        (expert_ids, route_weights, cotangent),
        **small,
    )
    mine, other, incoming = run_kernel(
        heads_kernel,
        [((chips, share, tokens), bf16)] * 2 + [((dh, dh), f32)],
        (place, arrived, queries, inner, grow, w_turned),
        smem=1,
        **small,
    )
    other = lax.ppermute(other, "exp", partner)
    pair = (mine.astype(f32) + other.astype(f32)).astype(bf16)
    pieces = lax.all_to_all(pair, "exp", 0, 0, axis_index_groups=same_core)
    residual, sent = run_kernel(
        send_kernel,
        [((tokens, share), bf16), ((n_exp, cap, 2 * share), bf16)],
        (pieces, resid, cot_parts, picks_turned),
        **small,
    )
    rows = lax.all_to_all(sent, "exp", 0, 0)
    packed, own, rstd = run_kernel(
        norm_kernel,
        [((n_ctx, 2 * cap, width), bf16), ((cap, width), bf16), ((cap, 128), f32)],
        (rows,),
        **small,
    )
    everyone = lax.all_to_all(packed, "ctx", 0, 0)
    [sums] = run_kernel(
        functools.partial(expert_kernel, step=256),
        [((n_ctx, 2 * cap, width), bf16)],
        (everyone, w_up[0], w_down[0]),
        flops=2_400_000_000,
        moved=11_000_000,
    )
    sums = lax.all_to_all(sums, "ctx", 0, 0)
    [returned] = run_kernel(
        back_kernel, [((n_exp, cap, 2 * share), bf16)], (sums, own, rstd), **small
    )
    returned = lax.all_to_all(returned, "exp", 0, 0)
    layer_out, resid_grad, turned_grad = run_kernel(
        join_kernel,
        [((tokens, share), bf16), ((tokens, share), bf16), ((share, tokens), bf16)],
        (returned, picks, route_weights, residual, cotangent),
        **small,
    )
    turned_grads = lax.all_gather(turned_grad, "exp", tiled=True)
    grad_heads, packed = run_kernel(
        state_grad_kernel,
        [(square, f32), ((n_ctx, dh, dh), bf16)],
        (turned_grads, w_out, queries, grow),
        **small,
    )
    states = lax.all_to_all(packed, "ctx", 0, 0)
    q_grad, k_part, v_part = run_kernel(
        grads_kernel,
        [(square, bf16), (square, f32), (square, f32)],
        (grad_heads, queries, keys, values, scores, decay, grow, incoming),
        **small,
    )
    k_grad, v_grad = run_kernel(
        last_kernel,
        [(square, bf16), (square, bf16)],
        (place, states, arrived, keys, values, keep, k_part, v_part),
        smem=1,
        **small,
    )
    return layer_out, resid_grad, q_grad, k_grad, v_grad


def solution(mesh):
    both = P("ctx", "exp")
    rows = P("ctx", None)
    return jax.shard_map(
        local,
        mesh=mesh,
        in_specs=(
            both, both, both, both, P("exp", "ctx"), P("exp", None),
            P("exp", None, "ctx"), P("exp", "ctx", None), rows, rows, both,
        ),
        out_specs=(both,) * 5,
        check_vma=False,
    )
```

```python
import functools

import jax
import jax.numpy as jnp
from jax import lax
from jax.experimental import pallas as pl
from jax.experimental.pallas import tpu as pltpu
from jax.sharding import PartitionSpec as P

bf16 = jnp.bfloat16
f32 = jnp.float32
ROWS = 16


def mm(a, b, dims):
    return lax.dot_general(a, b, (dims, ((), ())), preferred_element_type=f32)


def mm_high(a, b, dims):
    return lax.dot_general(
        a, b, (dims, ((), ())), precision=lax.Precision.HIGHEST, preferred_element_type=f32
    )


def iota(shape, axis):
    return lax.broadcasted_iota(jnp.int32, shape, axis)


def turned(column):
    n = column.shape[0]
    return jnp.sum(jnp.where(iota((n, n), 0) == iota((n, n), 1), column, 0.0), axis=0, keepdims=True)


def run_kernel(body, outs, args, smem=0, raw=0, flops=10_000_000, moved=1_000_000, limit=24):
    vmem = pl.BlockSpec(memory_space=pltpu.VMEM)
    scalars = [pl.BlockSpec(memory_space=pltpu.SMEM)] * smem
    specs = scalars + [pl.BlockSpec()] * raw + [vmem] * (len(args) - smem - raw)
    return pl.pallas_call(
        body,
        out_shape=[jax.ShapeDtypeStruct(shape, dtype) for shape, dtype in outs],
        in_specs=specs,
        out_specs=[vmem] * len(outs),
        compiler_params=pltpu.CompilerParams(vmem_limit_bytes=limit << 20),
        cost_estimate=pl.CostEstimate(flops=flops, bytes_accessed=moved, transcendentals=0),
    )(*args)


def pack(left, right):
    both = jnp.concatenate([left, right], axis=2)
    lanes, half = 128, both.shape[1] // 2
    rest = both[:, :, lanes:]
    rest = jnp.concatenate([rest[:, :half], rest[:, half:]], axis=2)
    return jnp.concatenate([both[:, :, :lanes], rest], axis=1)


def unpack(rows, share):
    lanes, half = 128, rows.shape[1] // 3
    top, low = rows[:, : 2 * half], rows[:, 2 * half :]
    rest = lanes // 2
    low = jnp.concatenate([low[:, :, :rest], low[:, :, rest:]], axis=1)
    both = jnp.concatenate([top, low], axis=2)
    return both[:, :, :share], both[:, :, share:]


def running(decay_row):
    n = decay_row.shape[1]
    causal = iota((n, n), 0) >= iota((n, n), 1)
    return jnp.sum(jnp.where(causal, decay_row, 0.0), axis=1, keepdims=True)


def state_kernel(keys, values, log_decay, packed):
    cum = running(log_decay[...])
    n = cum.shape[0]
    last = cum[n - 1 :, :]
    kept = keys[...].astype(f32) * jnp.exp(last - cum)
    state = mm_high(kept, values[...].astype(f32), ((0,), (0,))).astype(bf16)
    dh = state.shape[1]
    high = last.astype(bf16).astype(f32)
    mid = (last - high).astype(bf16).astype(f32)
    low = last - high - mid
    row = iota((ROWS, dh), 0)
    tail = jnp.where(row == 0, high, jnp.where(row == 1, mid, jnp.where(row == 2, low, 0.0)))
    for block in range(packed.shape[0]):
        packed[block, :dh, :] = state
        packed[block, dh:, :] = tail.astype(bf16)


def inner_kernel(queries, keys, values, log_decay, w_out, scores, inner, decay, grow, keep, w_turned):
    cum = running(log_decay[...])
    n = cum.shape[0]
    causal = iota((n, n), 0) >= iota((n, n), 1)
    gaps = jnp.where(causal, cum - turned(cum), 0.0)
    fall = jnp.where(causal, jnp.exp(gaps), 0.0)
    pairs = mm_high(queries[...].astype(f32), keys[...].astype(f32), ((1,), (1,))) * fall
    scores[...] = pairs
    decay[...] = fall
    inner[...] = mm_high(pairs, values[...].astype(f32), ((1,), (0,)))
    grow[...] = jnp.broadcast_to(jnp.exp(cum), grow.shape)
    keep[...] = jnp.broadcast_to(jnp.exp(cum[n - 1 :, :] - cum), keep.shape)
    dh = w_out.shape[0]
    for start in range(0, w_out.shape[1], dh):
        w_turned[start : start + dh, :] = w_out[:, start : start + dh].astype(f32).T.astype(bf16)


def route_kernel(ids, weights, cotangent, picks, cot_parts, *, cap):
    _, tokens = ids.shape
    slots_all = picks.shape[0]
    experts = slots_all // cap
    chosen = [(ids[j : j + 1, :] == iota((experts, tokens), 0)).astype(f32) for j in range(2)]
    earlier = (iota((tokens, tokens), 0) < iota((tokens, tokens), 1)).astype(f32).astype(bf16)
    before = mm((chosen[0] + chosen[1]).astype(bf16), earlier, ((1,), (0,)))
    cot = cotangent[...].astype(f32)
    for j in range(2):
        slot = jnp.sum(before * chosen[j], axis=0, keepdims=True)
        position = ids[j : j + 1, :].astype(f32) * cap + slot
        down = iota((slots_all, tokens), 0).astype(f32)
        at = slice(j * tokens, (j + 1) * tokens)
        picks[:, at] = (position == down).astype(f32).astype(bf16)
        cot_parts[:, at] = (weights[j : j + 1, :] * cot).astype(bf16)


def heads_kernel(place, queries, arrived, inner, grow, w_turned, mine, other, incoming):
    me, core = place[0], lax.rem(place[1], 2)
    blocks = arrived.shape[0]
    dh = queries.shape[1]
    total = jnp.zeros((dh, dh), f32)
    gap = jnp.zeros((1, dh), f32)
    for block in reversed(range(blocks)):
        weight = jnp.where(block < me, jnp.exp(gap), 0.0)
        total = total + weight * arrived[block, :dh, :].astype(f32)
        last = jnp.sum(arrived[block, dh:, :].astype(f32), axis=0, keepdims=True)
        gap = gap + jnp.where(block < me, last, 0.0)
    incoming[...] = total
    outer = mm_high(queries[...].astype(f32), total, ((1,), (0,)))
    heads = (inner[...] + grow[...] * outer).astype(bf16)
    chips, share, _ = mine.shape
    partial = mm(w_turned[...], heads, ((1,), (1,))).astype(bf16)
    partial = partial.reshape(chips, 2, share, heads.shape[0])
    mine[...] = jnp.where(core == 0, partial[:, 0], partial[:, 1])
    other[...] = jnp.where(core == 0, partial[:, 1], partial[:, 0])


def send_kernel(resid, pieces, cot_parts, picks, residual, sent):
    attn = jnp.sum(pieces[...].astype(f32), axis=0).astype(bf16).astype(f32)
    total = (resid[...].astype(f32) + attn).astype(bf16)
    residual[...] = total
    tokens = total.shape[1]
    placed = picks[:, :tokens] + picks[:, tokens:]
    share = total.shape[0]
    experts, rows_each, _ = sent.shape
    cap = picks.shape[0] // experts
    rows = mm(placed, total, ((1,), (1,))).reshape(experts, cap, share)
    grads = mm(picks[...], cot_parts[...], ((1,), (1,))).reshape(experts, cap, share)
    sent[...] = pack(rows, grads).astype(bf16)


def norm_kernel(rows, packed, own, rstd_out):
    experts = rows.shape[0]
    blocks, both, width = packed.shape
    cap, share = both // 2, width // experts
    left, right = unpack(rows[...].astype(f32), share)
    whole = jnp.concatenate([left[e] for e in range(experts)], axis=1)
    grads = jnp.concatenate([right[e] for e in range(experts)], axis=1).astype(bf16)
    rstd = lax.rsqrt(jnp.sum(whole * whole, axis=1, keepdims=True) / width + 1e-6)
    own[...] = whole.astype(bf16)
    rstd_out[...] = jnp.broadcast_to(rstd, rstd_out.shape)
    normed = (whole * rstd).astype(bf16)
    for block in range(blocks):
        packed[block, :cap, :] = normed
        packed[block, cap:, :] = grads


def expert_kernel(w_up, w_down, everyone, sums, *, step):
    blocks, both, width = everyone.shape
    cap = both // 2
    rows = blocks * cap
    hidden = w_up.shape[1]
    upper = jnp.zeros((rows, hidden), f32)
    grad_act = jnp.zeros((rows, hidden), f32)
    for start in range(0, width, step):
        at = slice(start, start + step)
        x = everyone[:, :cap, at].reshape(rows, step)
        g = everyone[:, cap:, at].reshape(rows, step)
        upper = upper + mm(x, w_up[at, :], ((1,), (0,)))
        grad_act = grad_act + mm(g, w_down[:, at], ((1,), (1,)))
    sigma = 1.0 / (1.0 + jnp.exp(-upper))
    act = (upper * sigma).astype(bf16)
    grad_up = (grad_act * (sigma * (1.0 + upper * (1.0 - sigma)))).astype(bf16)
    for start in range(0, width, step):
        at = slice(start, start + step)
        out = mm(act, w_down[:, at], ((1,), (0,))).astype(bf16)
        back = mm(grad_up, w_up[at, :], ((1,), (1,))).astype(bf16)
        sums[:, :cap, at] = out.reshape(blocks, cap, step)
        sums[:, cap:, at] = back.reshape(blocks, cap, step)


def back_kernel(sums, own, rstd_in, returned):
    experts = returned.shape[0]
    total = jnp.sum(sums[...].astype(f32), axis=0)
    cap, width = own.shape
    share = width // experts
    out, grads = total[:cap], total[cap:].astype(bf16).astype(f32)
    rows = own[...].astype(f32)
    rstd = rstd_in[:, :1]
    inner = jnp.sum(grads * rows, axis=1, keepdims=True)
    grads = rstd * grads - rows * (rstd * rstd * rstd * inner / width)
    left = jnp.stack([out[:, e * share : (e + 1) * share] for e in range(experts)])
    right = jnp.stack([grads[:, e * share : (e + 1) * share] for e in range(experts)])
    returned[...] = pack(left, right).astype(bf16)


def join_kernel(returned, picks, weights, residual, cotangent, layer_out, resid_grad):
    share, tokens = residual.shape
    slots_all = picks.shape[0]
    left, right = unpack(returned[...].astype(f32), share)
    left = left.reshape(slots_all, share).astype(bf16)
    right = right.reshape(slots_all, share).astype(bf16)
    both = mm(left, picks[...], ((0,), (0,)))
    routed = weights[0:1, :] * both[:, :tokens] + weights[1:2, :] * both[:, tokens:]
    layer_out[...] = (residual[...].astype(f32) + routed).astype(bf16)
    placed = picks[:, :tokens] + picks[:, tokens:]
    summed = mm(right, placed, ((0,), (0,)))
    resid_grad[...] = (cotangent[...].astype(f32) + summed).astype(bf16)


def state_grad_kernel(w_out, queries, turned_grads, grow, grad_heads, packed):
    flipped = mm(w_out[...], turned_grads[...], ((1,), (0,)))
    grads = flipped.T
    grad_heads[...] = grads
    state = mm_high(queries[...].astype(f32) * grow[...], grads, ((0,), (0,))).astype(bf16)
    for block in range(packed.shape[0]):
        packed[block] = state


def grads_kernel(
    queries, keys, values, grad_heads, scores, decay, grow, incoming, q_grad, k_part, v_part
):
    grads = grad_heads[...]
    score_grad = mm_high(grads, values[...].astype(f32), ((1,), (1,))) * decay[...]
    direct = mm_high(score_grad, keys[...].astype(f32), ((1,), (0,)))
    carried = mm_high(grads, incoming[...], ((1,), (1,)))
    q_grad[...] = (direct + grow[...] * carried).astype(bf16)
    k_part[...] = mm_high(score_grad, queries[...].astype(f32), ((0,), (0,)))
    v_part[...] = mm_high(scores[...], grads, ((0,), (0,)))


def last_kernel(place, keys, values, arrived, tails, keep, k_part, v_part, k_grad, v_grad):
    me = place[0]
    blocks, dh, _ = arrived.shape
    total = jnp.zeros((dh, dh), f32)
    gap = jnp.zeros((1, dh), f32)
    for block in range(blocks):
        weight = jnp.where(block > me, jnp.exp(gap), 0.0)
        total = total + weight * arrived[block].astype(f32)
        last = jnp.sum(tails[block, dh:, :].astype(f32), axis=0, keepdims=True)
        gap = gap + jnp.where(block > me, last, 0.0)
    from_values = mm_high(values[...].astype(f32), total, ((1,), (1,)))
    from_keys = mm_high(keys[...].astype(f32), total, ((1,), (0,)))
    k_grad[...] = (k_part[...] + keep[...] * from_values).astype(bf16)
    v_grad[...] = (v_part[...] + keep[...] * from_keys).astype(bf16)


def local(
    resid, queries, keys, values, log_decay, w_out, w_up, w_down, expert_ids, route_weights, cotangent
):
    n_ctx, n_exp = lax.axis_size("ctx"), lax.axis_size("exp")
    chips = n_exp // 2
    place = jnp.stack([lax.axis_index("ctx"), lax.axis_index("exp")]).astype(jnp.int32)
    tokens, dh = queries.shape
    width = w_out.shape[1]
    share = width // n_exp
    cap = 4 * tokens // n_exp
    partner = [(i, i ^ 1) for i in range(n_exp)]
    same_core = [[2 * z + c for z in range(chips)] for c in range(2)]
    square = (tokens, dh)
    flat = (share, tokens)
    weights, cot = route_weights.T, cotangent.T
    packed_rows = (n_exp, cap * 2 * share // 128, 128)

    [packed] = run_kernel(
        state_kernel, [((n_ctx, dh + ROWS, dh), bf16)], (keys, values, log_decay), raw=3
    )
    arrived = lax.all_to_all(packed, "ctx", 0, 0)
    scores, inner, decay, grow, keep, w_turned = run_kernel(
        inner_kernel,
        [((tokens, tokens), f32), (square, f32), ((tokens, tokens), f32), (square, f32), (square, f32)]
        + [((width, dh), bf16)],
        (queries, keys, values, log_decay, w_out),
        raw=5,
    )
    picks, cot_parts = run_kernel(
        functools.partial(route_kernel, cap=cap),
        [((n_exp * cap, 2 * tokens), bf16), ((share, 2 * tokens), bf16)],
        (expert_ids.T, weights, cot),
        raw=3,
    )
    mine, other, incoming = run_kernel(
        heads_kernel,
        [((chips, share, tokens), bf16)] * 2 + [((dh, dh), f32)],
        (place, queries, arrived, inner, grow, w_turned),
        smem=1,
        raw=1,
    )
    other = lax.ppermute(other, "exp", partner)
    pair = (mine.astype(f32) + other.astype(f32)).astype(bf16)
    pieces = lax.all_to_all(pair, "exp", 0, 0, axis_index_groups=same_core)
    residual, sent = run_kernel(
        send_kernel,
        [(flat, bf16), (packed_rows, bf16)],
        (resid.T, pieces, cot_parts, picks),
        raw=1,
    )
    rows = lax.all_to_all(sent, "exp", 0, 0)
    packed, own, rstd = run_kernel(
        norm_kernel,
        [((n_ctx, 2 * cap, width), bf16), ((cap, width), bf16), ((cap, 128), f32)],
        (rows,),
    )
    everyone = lax.all_to_all(packed, "ctx", 0, 0)
    [sums] = run_kernel(
        functools.partial(expert_kernel, step=512 if width % 512 == 0 else 384),
        [((n_ctx, 2 * cap, width), bf16)],
        (w_up[0], w_down[0], everyone),
        flops=2_400_000_000,
        moved=11_000_000,
    )
    sums = lax.all_to_all(sums, "ctx", 0, 0)
    [returned] = run_kernel(back_kernel, [(packed_rows, bf16)], (sums, own, rstd))
    returned = lax.all_to_all(returned, "exp", 0, 0)
    layer_out, resid_grad = run_kernel(
        join_kernel,
        [(flat, bf16), (flat, bf16)],
        (returned, picks, weights, residual, cot),
    )
    turned_grads = lax.all_gather(resid_grad, "exp", tiled=True)
    grad_heads, packed = run_kernel(
        state_grad_kernel,
        [(square, f32), ((n_ctx, dh, dh), bf16)],
        (w_out, queries, turned_grads, grow),
    )
    states = lax.all_to_all(packed, "ctx", 0, 0)
    q_grad, k_part, v_part = run_kernel(
        grads_kernel,
        [(square, bf16), (square, f32), (square, f32)],
        (queries, keys, values, grad_heads, scores, decay, grow, incoming),
    )
    k_grad, v_grad = run_kernel(
        last_kernel,
        [(square, bf16), (square, bf16)],
        (place, keys, values, states, arrived, keep, k_part, v_part),
        smem=1,
    )
    return layer_out.T, resid_grad.T, q_grad, k_grad, v_grad


def solution(mesh):
    both = P("ctx", "exp")
    rows = P("ctx", None)
    return jax.shard_map(
        local,
        mesh=mesh,
        in_specs=(
            both, both, both, both, P("exp", "ctx"), P("exp", None),
            P("exp", None, "ctx"), P("exp", "ctx", None), rows, rows, both,
        ),
        out_specs=(both,) * 5,
        check_vma=False,
    )
```

```python
import functools
import math

import jax
import jax.numpy as jnp
from jax import lax
from jax.experimental import pallas as pl
from jax.experimental.pallas import tpu as pltpu
from jax.sharding import PartitionSpec as P

bf16 = jnp.bfloat16
f32 = jnp.float32
ROWS = 16


def mm(a, b, dims):
    return lax.dot_general(a, b, (dims, ((), ())), preferred_element_type=f32)


def mm_high(a, b, dims):
    return lax.dot_general(
        a, b, (dims, ((), ())), precision=lax.Precision.HIGHEST, preferred_element_type=f32
    )


def iota(shape, axis):
    return lax.broadcasted_iota(jnp.int32, shape, axis)


def turned(column):
    n = column.shape[0]
    return jnp.sum(jnp.where(iota((n, n), 0) == iota((n, n), 1), column, 0.0), axis=0, keepdims=True)


def run_kernel(
    body, outs, args, smem=0, raw=0, far=0, scratch=(), flops=10_000_000, moved=1_000_000, limit=24
):
    vmem = pl.BlockSpec(memory_space=pltpu.VMEM)
    scalars = [pl.BlockSpec(memory_space=pltpu.SMEM)] * smem
    hbm = pl.BlockSpec(memory_space=pltpu.HBM)
    near = len(args) - smem - far - raw
    specs = scalars + [hbm] * far + [pl.BlockSpec()] * raw + [vmem] * near
    return pl.pallas_call(
        body,
        out_shape=[jax.ShapeDtypeStruct(shape, dtype) for shape, dtype in outs],
        in_specs=specs,
        out_specs=[vmem] * len(outs),
        scratch_shapes=scratch,
        compiler_params=pltpu.CompilerParams(vmem_limit_bytes=limit << 20),
        cost_estimate=pl.CostEstimate(flops=flops, bytes_accessed=moved, transcendentals=0),
    )(*args)


def pack(left, right):
    both = jnp.concatenate([left, right], axis=2)
    lanes, half = 128, both.shape[1] // 2
    rest = both[:, :, lanes:]
    rest = jnp.concatenate([rest[:, :half], rest[:, half:]], axis=2)
    return jnp.concatenate([both[:, :, :lanes], rest], axis=1)


def unpack(rows, share):
    lanes, half = 128, rows.shape[1] // 3
    top, low = rows[:, : 2 * half], rows[:, 2 * half :]
    rest = lanes // 2
    low = jnp.concatenate([low[:, :, :rest], low[:, :, rest:]], axis=1)
    both = jnp.concatenate([top, low], axis=2)
    return both[:, :, :share], both[:, :, share:]


def running(decay_row):
    n = decay_row.shape[1]
    causal = iota((n, n), 0) >= iota((n, n), 1)
    return jnp.sum(jnp.where(causal, decay_row, 0.0), axis=1, keepdims=True)


def state_kernel(keys_far, values_far, decay_far, packed, keys, values, log_decay, arrivals):
    pairs = ((keys_far, keys), (values_far, values), (decay_far, log_decay))
    copies = [pltpu.make_async_copy(a, b, arrivals.at[i]) for i, (a, b) in enumerate(pairs)]
    for copy in copies:
        copy.start()
    for copy in copies:
        copy.wait()
    cum = running(log_decay[...])
    n = cum.shape[0]
    last = cum[n - 1 :, :]
    kept = keys[...].astype(f32) * jnp.exp(last - cum)
    state = mm_high(kept, values[...].astype(f32), ((0,), (0,))).astype(bf16)
    dh = state.shape[1]
    high = last.astype(bf16).astype(f32)
    mid = (last - high).astype(bf16).astype(f32)
    low = last - high - mid
    row = iota((ROWS, dh), 0)
    tail = jnp.where(row == 0, high, jnp.where(row == 1, mid, jnp.where(row == 2, low, 0.0)))
    for block in range(packed.shape[0]):
        packed[block, :dh, :] = state
        packed[block, dh:, :] = tail.astype(bf16)


def inner_kernel(queries, keys, values, log_decay, w_out, scores, inner, decay, grow, keep, grown, w_turned):
    cum = running(log_decay[...])
    n = cum.shape[0]
    causal = iota((n, n), 0) >= iota((n, n), 1)
    gaps = jnp.where(causal, cum - turned(cum), 0.0)
    fall = jnp.where(causal, jnp.exp(gaps), 0.0)
    pairs = mm_high(queries[...].astype(f32), keys[...].astype(f32), ((1,), (1,))) * fall
    scores[...] = pairs
    decay[...] = fall
    inner[...] = mm_high(pairs, values[...].astype(f32), ((1,), (0,)))
    grow[...] = jnp.broadcast_to(jnp.exp(cum), grow.shape)
    grown[...] = queries[...].astype(f32) * jnp.exp(cum)
    keep[...] = jnp.broadcast_to(jnp.exp(cum[n - 1 :, :] - cum), keep.shape)
    dh = w_out.shape[0]
    for start in range(0, w_out.shape[1], dh):
        w_turned[start : start + dh, :] = w_out[:, start : start + dh].astype(f32).T.astype(bf16)


def route_kernel(ids, weights, cotangent, picks, cot_parts, *, cap):
    _, tokens = ids.shape
    slots_all = picks.shape[0]
    experts = slots_all // cap
    chosen = [(ids[j : j + 1, :] == iota((experts, tokens), 0)).astype(f32) for j in range(2)]
    earlier = (iota((tokens, tokens), 0) < iota((tokens, tokens), 1)).astype(f32).astype(bf16)
    before = mm((chosen[0] + chosen[1]).astype(bf16), earlier, ((1,), (0,)))
    cot = cotangent[...].astype(f32)
    for j in range(2):
        slot = jnp.sum(before * chosen[j], axis=0, keepdims=True)
        position = ids[j : j + 1, :].astype(f32) * cap + slot
        down = iota((slots_all, tokens), 0).astype(f32)
        at = slice(j * tokens, (j + 1) * tokens)
        picks[:, at] = (position == down).astype(f32).astype(bf16)
        cot_parts[:, at] = (weights[j : j + 1, :] * cot).astype(bf16)


def heads_kernel(place, arrived, inner, grown, w_turned, mine, other, incoming):
    me, core = place[0], lax.rem(place[1], 2)
    blocks = arrived.shape[0]
    dh = grown.shape[1]
    total = jnp.zeros((dh, dh), f32)
    gap = jnp.zeros((1, dh), f32)
    for block in reversed(range(blocks)):
        weight = jnp.where(block < me, jnp.exp(gap), 0.0)
        total = total + weight * arrived[block, :dh, :].astype(f32)
        last = jnp.sum(arrived[block, dh:, :].astype(f32), axis=0, keepdims=True)
        gap = gap + jnp.where(block < me, last, 0.0)
    incoming[...] = total
    heads = (inner[...] + mm_high(grown[...], total, ((1,), (0,)))).astype(bf16)
    chips, share, _ = mine.shape
    partial = mm(w_turned[...], heads, ((1,), (1,))).astype(bf16)
    partial = partial.reshape(chips, 2, share, heads.shape[0])
    mine[...] = jnp.where(core == 0, partial[:, 0], partial[:, 1])
    other[...] = jnp.where(core == 0, partial[:, 1], partial[:, 0])


def send_kernel(resid, pieces, cot_parts, picks, residual, sent):
    attn = jnp.sum(pieces[...].astype(f32), axis=0).astype(bf16).astype(f32)
    total = (resid[...].astype(f32) + attn).astype(bf16)
    residual[...] = total
    tokens = total.shape[1]
    placed = picks[:, :tokens] + picks[:, tokens:]
    share = total.shape[0]
    experts, rows_each, _ = sent.shape
    cap = picks.shape[0] // experts
    rows = mm(placed, total, ((1,), (1,))).reshape(experts, cap, share)
    grads = mm(picks[...], cot_parts[...], ((1,), (1,))).reshape(experts, cap, share)
    sent[...] = pack(rows, grads).astype(bf16)


def norm_kernel(rows, packed, own, rstd_out):
    experts = rows.shape[0]
    blocks, both, width = packed.shape
    cap, share = both // 2, width // experts
    left, right = unpack(rows[...].astype(f32), share)
    whole = jnp.concatenate([left[e] for e in range(experts)], axis=1)
    grads = jnp.concatenate([right[e] for e in range(experts)], axis=1).astype(bf16)
    rstd = lax.rsqrt(jnp.sum(whole * whole, axis=1, keepdims=True) / width + 1e-6)
    own[...] = whole.astype(bf16)
    rstd_out[...] = jnp.broadcast_to(rstd, rstd_out.shape)
    normed = (whole * rstd).astype(bf16)
    for block in range(blocks):
        packed[block, :cap, :] = normed
        packed[block, cap:, :] = grads


def expert_kernel(w_up, w_down, everyone, sums, *, step):
    blocks, both, width = everyone.shape
    cap = both // 2
    rows = blocks * cap
    hidden = w_up.shape[1]
    upper = jnp.zeros((rows, hidden), f32)
    grad_act = jnp.zeros((rows, hidden), f32)
    for start in range(0, width, step):
        at = slice(start, start + step)
        x = everyone[:, :cap, at].reshape(rows, step)
        g = everyone[:, cap:, at].reshape(rows, step)
        upper = upper + mm(x, w_up[at, :], ((1,), (0,)))
        grad_act = grad_act + mm(g, w_down[:, at], ((1,), (1,)))
    sigma = 1.0 / (1.0 + jnp.exp(-upper))
    act = (upper * sigma).astype(bf16)
    grad_up = (grad_act * (sigma * (1.0 + upper * (1.0 - sigma)))).astype(bf16)
    for start in range(0, width, step):
        at = slice(start, start + step)
        out = mm(act, w_down[:, at], ((1,), (0,))).astype(bf16)
        back = mm(grad_up, w_up[at, :], ((1,), (1,))).astype(bf16)
        sums[:, :cap, at] = out.reshape(blocks, cap, step)
        sums[:, cap:, at] = back.reshape(blocks, cap, step)


def half_kernel(sums, out, *, step):
    for start in range(0, out.shape[2], step):
        at = slice(start, start + step)
        total = jnp.sum(sums[:, :, at].astype(f32), axis=0).astype(bf16)
        out[:, :, at] = total.reshape(out.shape[0], out.shape[1], step)


def back_kernel(sums, own, rstd_in, returned):
    experts = returned.shape[0]
    total = jnp.sum(sums[...].astype(f32), axis=0)
    cap, width = own.shape
    share = width // experts
    out, grads = total[:cap], total[cap:].astype(bf16).astype(f32)
    rows = own[...].astype(f32)
    rstd = rstd_in[:, :1]
    inner = jnp.sum(grads * rows, axis=1, keepdims=True)
    grads = rstd * grads - rows * (rstd * rstd * rstd * inner / width)
    left = jnp.stack([out[:, e * share : (e + 1) * share] for e in range(experts)])
    right = jnp.stack([grads[:, e * share : (e + 1) * share] for e in range(experts)])
    returned[...] = pack(left, right).astype(bf16)


def join_kernel(returned, picks, weights, residual, cotangent, layer_out, resid_grad):
    share, tokens = residual.shape
    slots_all = picks.shape[0]
    left, right = unpack(returned[...].astype(f32), share)
    left = left.reshape(slots_all, share).astype(bf16)
    right = right.reshape(slots_all, share).astype(bf16)
    both = mm(left, picks[...], ((0,), (0,)))
    routed = weights[0:1, :] * both[:, :tokens] + weights[1:2, :] * both[:, tokens:]
    layer_out[...] = (residual[...].astype(f32) + routed).astype(bf16)
    placed = picks[:, :tokens] + picks[:, tokens:]
    summed = mm(right, placed, ((0,), (0,)))
    resid_grad[...] = (cotangent[...].astype(f32) + summed).astype(bf16)


def state_grad_kernel(w_out, turned_grads, grown, grad_heads, packed):
    flipped = mm(w_out[...], turned_grads[...], ((1,), (0,)))
    grads = flipped.T
    grad_heads[...] = grads
    state = mm_high(grown[...], grads, ((0,), (0,))).astype(bf16)
    for block in range(packed.shape[0]):
        packed[block] = state


def grads_kernel(
    queries, keys, values, grad_heads, scores, decay, grow, incoming, q_grad, k_part, v_part
):
    grads = grad_heads[...]
    score_grad = mm_high(grads, values[...].astype(f32), ((1,), (1,))) * decay[...]
    direct = mm_high(score_grad, keys[...].astype(f32), ((1,), (0,)))
    carried = mm_high(grads, incoming[...], ((1,), (1,)))
    q_grad[...] = (direct + grow[...] * carried).astype(bf16)
    k_part[...] = mm_high(score_grad, queries[...].astype(f32), ((0,), (0,)))
    v_part[...] = mm_high(scores[...], grads, ((0,), (0,)))


def last_kernel(place, keys, values, arrived, tails, keep, k_part, v_part, k_grad, v_grad):
    me = place[0]
    blocks, dh, _ = arrived.shape
    total = jnp.zeros((dh, dh), f32)
    gap = jnp.zeros((1, dh), f32)
    for block in range(blocks):
        weight = jnp.where(block > me, jnp.exp(gap), 0.0)
        total = total + weight * arrived[block].astype(f32)
        last = jnp.sum(tails[block, dh:, :].astype(f32), axis=0, keepdims=True)
        gap = gap + jnp.where(block > me, last, 0.0)
    from_values = mm_high(values[...].astype(f32), total, ((1,), (1,)))
    from_keys = mm_high(keys[...].astype(f32), total, ((1,), (0,)))
    k_grad[...] = (k_part[...] + keep[...] * from_values).astype(bf16)
    v_grad[...] = (v_part[...] + keep[...] * from_keys).astype(bf16)


def local(
    resid, queries, keys, values, log_decay, w_out, w_up, w_down, expert_ids, route_weights, cotangent
):
    n_ctx, n_exp = lax.axis_size("ctx"), lax.axis_size("exp")
    chips = n_exp // 2
    place = jnp.stack([lax.axis_index("ctx"), lax.axis_index("exp")]).astype(jnp.int32)
    tokens, dh = queries.shape
    width = w_out.shape[1]
    share = width // n_exp
    cap = 4 * tokens // n_exp
    partner = [(i, i ^ 1) for i in range(n_exp)]
    same_core = [[2 * z + c for z in range(chips)] for c in range(2)]
    side = math.isqrt(n_ctx)
    axes = ("ctx", "exp")
    first, second = [], []
    for e in range(n_exp):
        along_y = [[(x * side + y) * n_exp + e for y in range(side)] for x in range(side)]
        along_x = [[(x * side + y) * n_exp + e for x in range(side)] for y in range(side)]
        first += along_x if e % 2 else along_y
        second += along_y if e % 2 else along_x
    square = (tokens, dh)
    flat = (share, tokens)
    weights, cot = route_weights.T, cotangent.T
    packed_rows = (n_exp, cap * 2 * share // 128, 128)

    [packed] = run_kernel(
        state_kernel,
        [((n_ctx, dh + ROWS, dh), bf16)],
        (keys, values, log_decay),
        far=3,
        scratch=[pltpu.VMEM(square, bf16)] * 2
        + [pltpu.VMEM(log_decay.shape, f32), pltpu.SemaphoreType.DMA((3,))],
    )
    arrived = lax.all_to_all(packed, "ctx", 0, 0)
    scores, inner, decay, grow, keep, grown, w_turned = run_kernel(
        inner_kernel,
        [((tokens, tokens), f32), (square, f32), ((tokens, tokens), f32), (square, f32), (square, f32)]
        + [(square, f32), ((width, dh), bf16)],
        (queries, keys, values, log_decay, w_out),
        raw=5,
    )
    picks, cot_parts = run_kernel(
        functools.partial(route_kernel, cap=cap),
        [((n_exp * cap, 2 * tokens), bf16), ((share, 2 * tokens), bf16)],
        (expert_ids.T, weights, cot),
        raw=3,
    )
    mine, other, incoming = run_kernel(
        heads_kernel,
        [((chips, share, tokens), bf16)] * 2 + [((dh, dh), f32)],
        (place, arrived, inner, grown, w_turned),
        smem=1,
    )
    other = lax.ppermute(other, "exp", partner)
    pair = (mine.astype(f32) + other.astype(f32)).astype(bf16)
    pieces = lax.all_to_all(pair, "exp", 0, 0, axis_index_groups=same_core)
    residual, sent = run_kernel(
        send_kernel,
        [(flat, bf16), (packed_rows, bf16)],
        (resid.T, pieces, cot_parts, picks),
        raw=1,
    )
    rows = lax.all_to_all(sent, "exp", 0, 0)
    packed, own, rstd = run_kernel(
        norm_kernel,
        [((side, 2 * cap, width), bf16), ((cap, width), bf16), ((cap, 128), f32)],
        (rows,),
    )
    line = lax.all_to_all(packed, axes, 0, 0, axis_index_groups=first)
    line = jnp.broadcast_to(line.reshape(1, side * 2 * cap, width), (side, side * 2 * cap, width))
    everyone = lax.all_to_all(line, axes, 0, 0, axis_index_groups=second)
    everyone = everyone.reshape(n_ctx, 2 * cap, width)
    [sums] = run_kernel(
        functools.partial(expert_kernel, step=512 if width % 512 == 0 else 384),
        [((n_ctx, 2 * cap, width), bf16)],
        (w_up[0], w_down[0], everyone),
        flops=2_400_000_000,
        moved=11_000_000,
    )
    sums = sums.reshape(side, side * 2 * cap, width)
    sums = lax.all_to_all(sums, axes, 0, 0, axis_index_groups=second)
    [sums] = run_kernel(
        functools.partial(half_kernel, step=128), [((side, 2 * cap, width), bf16)], (sums,)
    )
    sums = lax.all_to_all(sums, axes, 0, 0, axis_index_groups=first)
    [returned] = run_kernel(back_kernel, [(packed_rows, bf16)], (sums, own, rstd))
    returned = lax.all_to_all(returned, "exp", 0, 0)
    layer_out, resid_grad = run_kernel(
        join_kernel,
        [(flat, bf16), (flat, bf16)],
        (returned, picks, weights, residual, cot),
    )
    turned_grads = lax.all_gather(resid_grad, "exp", tiled=True)
    grad_heads, packed = run_kernel(
        state_grad_kernel,
        [(square, f32), ((n_ctx, dh, dh), bf16)],
        (w_out, turned_grads, grown),
    )
    states = lax.all_to_all(packed, "ctx", 0, 0)
    q_grad, k_part, v_part = run_kernel(
        grads_kernel,
        [(square, bf16), (square, f32), (square, f32)],
        (queries, keys, values, grad_heads, scores, decay, grow, incoming),
    )
    k_grad, v_grad = run_kernel(
        last_kernel,
        [(square, bf16), (square, bf16)],
        (place, keys, values, states, arrived, keep, k_part, v_part),
        smem=1,
    )
    return layer_out.T, resid_grad.T, q_grad, k_grad, v_grad


def solution(mesh):
    both = P("ctx", "exp")
    rows = P("ctx", None)
    return jax.shard_map(
        local,
        mesh=mesh,
        in_specs=(
            both, both, both, both, P("exp", "ctx"), P("exp", None),
            P("exp", None, "ctx"), P("exp", "ctx", None), rows, rows, both,
        ),
        out_specs=(both,) * 5,
        check_vma=False,
    )
```

```python
import functools
import math

import jax
import jax.numpy as jnp
from jax import lax
from jax.experimental import pallas as pl
from jax.experimental.pallas import tpu as pltpu
from jax.sharding import PartitionSpec as P

bf16 = jnp.bfloat16
f32 = jnp.float32
ROWS = 16


def mm(a, b, dims):
    return lax.dot_general(a, b, (dims, ((), ())), preferred_element_type=f32)


def mm_high(a, b, dims):
    return lax.dot_general(
        a, b, (dims, ((), ())), precision=lax.Precision.HIGHEST, preferred_element_type=f32
    )


def iota(shape, axis):
    return lax.broadcasted_iota(jnp.int32, shape, axis)


def turned(column):
    n = column.shape[0]
    return jnp.sum(jnp.where(iota((n, n), 0) == iota((n, n), 1), column, 0.0), axis=0, keepdims=True)


def run_kernel(
    body, outs, args, smem=0, raw=0, far=0, scratch=(), flops=10_000_000, moved=1_000_000, limit=24
):
    vmem = pl.BlockSpec(memory_space=pltpu.VMEM)
    scalars = [pl.BlockSpec(memory_space=pltpu.SMEM)] * smem
    hbm = pl.BlockSpec(memory_space=pltpu.HBM)
    near = len(args) - smem - far - raw
    specs = scalars + [hbm] * far + [pl.BlockSpec()] * raw + [vmem] * near
    return pl.pallas_call(
        body,
        out_shape=[jax.ShapeDtypeStruct(shape, dtype) for shape, dtype in outs],
        in_specs=specs,
        out_specs=[vmem] * len(outs),
        scratch_shapes=scratch,
        compiler_params=pltpu.CompilerParams(vmem_limit_bytes=limit << 20),
        cost_estimate=pl.CostEstimate(flops=flops, bytes_accessed=moved, transcendentals=0),
    )(*args)


def pack(left, right):
    both = jnp.concatenate([left, right], axis=2)
    lanes, half = 128, both.shape[1] // 2
    rest = both[:, :, lanes:]
    rest = jnp.concatenate([rest[:, :half], rest[:, half:]], axis=2)
    return jnp.concatenate([both[:, :, :lanes], rest], axis=1)


def unpack(rows, share):
    lanes, half = 128, rows.shape[1] // 3
    top, low = rows[:, : 2 * half], rows[:, 2 * half :]
    rest = lanes // 2
    low = jnp.concatenate([low[:, :, :rest], low[:, :, rest:]], axis=1)
    both = jnp.concatenate([top, low], axis=2)
    return both[:, :, :share], both[:, :, share:]


def running(decay_row):
    n = decay_row.shape[1]
    causal = iota((n, n), 0) >= iota((n, n), 1)
    return jnp.sum(jnp.where(causal, decay_row, 0.0), axis=1, keepdims=True)


def state_kernel(keys_far, values_far, decay_far, packed, keys, values, log_decay, arrivals):
    pairs = ((keys_far, keys), (values_far, values), (decay_far, log_decay))
    copies = [pltpu.make_async_copy(a, b, arrivals.at[i]) for i, (a, b) in enumerate(pairs)]
    for copy in copies:
        copy.start()
    for copy in copies:
        copy.wait()
    cum = running(log_decay[...])
    n = cum.shape[0]
    last = cum[n - 1 :, :]
    kept = keys[...].astype(f32) * jnp.exp(last - cum)
    state = mm_high(kept, values[...].astype(f32), ((0,), (0,))).astype(bf16)
    dh = state.shape[1]
    high = last.astype(bf16).astype(f32)
    mid = (last - high).astype(bf16).astype(f32)
    low = last - high - mid
    row = iota((ROWS, dh), 0)
    tail = jnp.where(row == 0, high, jnp.where(row == 1, mid, jnp.where(row == 2, low, 0.0)))
    for block in range(packed.shape[0]):
        packed[block, :dh, :] = state
        packed[block, dh:, :] = tail.astype(bf16)


def inner_kernel(
    place, log_decay, w_out, heads_in, scores, inner, decay, grow, keep, grown, mine, theirs
):
    cum = running(log_decay[...])
    n = cum.shape[0]
    causal = iota((n, n), 0) >= iota((n, n), 1)
    gaps = jnp.where(causal, cum - turned(cum), 0.0)
    fall = jnp.where(causal, jnp.exp(gaps), 0.0)
    pairs = mm_high(heads_in[0].astype(f32), heads_in[1].astype(f32), ((1,), (1,))) * fall
    scores[...] = pairs
    decay[...] = fall
    inner[...] = mm_high(pairs, heads_in[2].astype(f32), ((1,), (0,)))
    grow[...] = jnp.broadcast_to(jnp.exp(cum), grow.shape)
    grown[...] = heads_in[0].astype(f32) * jnp.exp(cum)
    keep[...] = jnp.broadcast_to(jnp.exp(cum[n - 1 :, :] - cum), keep.shape)
    dh, width = w_out.shape
    chips, share, _ = mine.shape
    blocks = [w_out[:, at : at + dh].astype(f32).T.astype(bf16) for at in range(0, width, dh)]
    flipped = jnp.concatenate(blocks, axis=0).reshape(chips, 2, share, dh)
    even = lax.rem(place[1], 2) == 0
    mine[...] = jnp.where(even, flipped[:, 0], flipped[:, 1])
    theirs[...] = jnp.where(even, flipped[:, 1], flipped[:, 0])


def route_kernel(ids, weights, cotangent, picks, cot_parts, *, cap):
    _, tokens = ids.shape
    slots_all = picks.shape[0]
    experts = slots_all // cap
    chosen = [(ids[j : j + 1, :] == iota((experts, tokens), 0)).astype(f32) for j in range(2)]
    earlier = (iota((tokens, tokens), 0) < iota((tokens, tokens), 1)).astype(f32).astype(bf16)
    before = mm((chosen[0] + chosen[1]).astype(bf16), earlier, ((1,), (0,)))
    cot = cotangent[...].astype(f32)
    for j in range(2):
        slot = jnp.sum(before * chosen[j], axis=0, keepdims=True)
        position = ids[j : j + 1, :].astype(f32) * cap + slot
        down = iota((slots_all, tokens), 0).astype(f32)
        at = slice(j * tokens, (j + 1) * tokens)
        picks[:, at] = (position == down).astype(f32).astype(bf16)
        cot_parts[:, at] = (weights[j : j + 1, :] * cot).astype(bf16)


def heads_kernel(place, arrived, inner, grown, heads, incoming):
    me = place[0]
    blocks = arrived.shape[0]
    dh = grown.shape[1]
    total = jnp.zeros((dh, dh), f32)
    gap = jnp.zeros((1, dh), f32)
    for block in reversed(range(blocks)):
        weight = jnp.where(block < me, jnp.exp(gap), 0.0)
        total = total + weight * arrived[block, :dh, :].astype(f32)
        last = jnp.sum(arrived[block, dh:, :].astype(f32), axis=0, keepdims=True)
        gap = gap + jnp.where(block < me, last, 0.0)
    incoming[...] = total
    heads[...] = (inner[...] + mm_high(grown[...], total, ((1,), (0,)))).astype(bf16)


def project_kernel(heads, heads_given, weights, weights_given, partial):
    chips, share, dh = weights.shape
    both = jnp.concatenate([weights[...], weights_given[...]], axis=2).reshape(chips * share, 2 * dh)
    pair = jnp.concatenate([heads[...], heads_given[...]], axis=1)
    partial[...] = mm(both, pair, ((1,), (1,))).astype(bf16).reshape(partial.shape)


def send_kernel(resid, pieces, cot_parts, picks, residual, sent):
    attn = jnp.sum(pieces[...].astype(f32), axis=0).astype(bf16).astype(f32)
    total = (resid[...].astype(f32) + attn).astype(bf16)
    residual[...] = total
    tokens = total.shape[1]
    placed = picks[:, :tokens] + picks[:, tokens:]
    share = total.shape[0]
    experts, rows_each, _ = sent.shape
    cap = picks.shape[0] // experts
    rows = mm(placed, total, ((1,), (1,))).reshape(experts, cap, share)
    grads = mm(picks[...], cot_parts[...], ((1,), (1,))).reshape(experts, cap, share)
    sent[...] = pack(rows, grads).astype(bf16)


def norm_kernel(rows, packed, own, rstd_out):
    experts = rows.shape[0]
    blocks, both, width = packed.shape
    cap, share = both // 2, width // experts
    left, right = unpack(rows[...].astype(f32), share)
    whole = jnp.concatenate([left[e] for e in range(experts)], axis=1)
    grads = jnp.concatenate([right[e] for e in range(experts)], axis=1).astype(bf16)
    rstd = lax.rsqrt(jnp.sum(whole * whole, axis=1, keepdims=True) / width + 1e-6)
    own[...] = whole.astype(bf16)
    rstd_out[...] = jnp.broadcast_to(rstd, rstd_out.shape)
    normed = (whole * rstd).astype(bf16)
    for block in range(blocks):
        packed[block, :cap, :] = normed
        packed[block, cap:, :] = grads


def expert_kernel(w_up, w_down, everyone, sums, *, step):
    blocks, both, width = everyone.shape
    cap = both // 2
    rows = blocks * cap
    hidden = w_up.shape[1]
    upper = jnp.zeros((rows, hidden), f32)
    grad_act = jnp.zeros((rows, hidden), f32)
    for start in range(0, width, step):
        at = slice(start, start + step)
        x = everyone[:, :cap, at].reshape(rows, step)
        g = everyone[:, cap:, at].reshape(rows, step)
        upper = upper + mm(x, w_up[at, :], ((1,), (0,)))
        grad_act = grad_act + mm(g, w_down[:, at], ((1,), (1,)))
    sigma = 1.0 / (1.0 + jnp.exp(-upper))
    act = (upper * sigma).astype(bf16)
    grad_up = (grad_act * (sigma * (1.0 + upper * (1.0 - sigma)))).astype(bf16)
    for start in range(0, width, step):
        at = slice(start, start + step)
        out = mm(act, w_down[:, at], ((1,), (0,))).astype(bf16)
        back = mm(grad_up, w_up[at, :], ((1,), (1,))).astype(bf16)
        sums[:, :cap, at] = out.reshape(blocks, cap, step)
        sums[:, cap:, at] = back.reshape(blocks, cap, step)


def half_kernel(sums, out, *, step):
    for start in range(0, out.shape[2], step):
        at = slice(start, start + step)
        total = jnp.sum(sums[:, :, at].astype(f32), axis=0).astype(bf16)
        out[:, :, at] = total.reshape(out.shape[0], out.shape[1], step)


def back_kernel(sums, own, rstd_in, returned):
    experts = returned.shape[0]
    total = jnp.sum(sums[...].astype(f32), axis=0)
    cap, width = own.shape
    share = width // experts
    out, grads = total[:cap], total[cap:].astype(bf16).astype(f32)
    rows = own[...].astype(f32)
    rstd = rstd_in[:, :1]
    inner = jnp.sum(grads * rows, axis=1, keepdims=True)
    grads = rstd * grads - rows * (rstd * rstd * rstd * inner / width)
    left = jnp.stack([out[:, e * share : (e + 1) * share] for e in range(experts)])
    right = jnp.stack([grads[:, e * share : (e + 1) * share] for e in range(experts)])
    returned[...] = pack(left, right).astype(bf16)


def join_kernel(returned, picks, weights, residual, cotangent, layer_out, resid_grad):
    share, tokens = residual.shape
    slots_all = picks.shape[0]
    left, right = unpack(returned[...].astype(f32), share)
    rows = jnp.concatenate([left, right], axis=2).reshape(slots_all, 2 * share).astype(bf16)
    all_rows = mm(rows, picks[...], ((0,), (0,)))
    both = all_rows[:share]
    routed = weights[0:1, :] * both[:, :tokens] + weights[1:2, :] * both[:, tokens:]
    layer_out[...] = (residual[...].astype(f32) + routed).astype(bf16)
    summed = all_rows[share:, :tokens] + all_rows[share:, tokens:]
    resid_grad[...] = (cotangent[...].astype(f32) + summed).astype(bf16)


def state_grad_kernel(w_out, turned_grads, grown, grad_heads, packed):
    flipped = mm(w_out[...], turned_grads[...], ((1,), (0,)))
    grads = flipped.T
    grad_heads[...] = grads
    state = mm_high(grown[...], grads, ((0,), (0,))).astype(bf16)
    for block in range(packed.shape[0]):
        packed[block] = state


def grads_kernel(
    heads_in, grad_heads, scores, decay, grow, incoming, q_grad, k_part, v_part
):
    grads = grad_heads[...]
    score_grad = mm_high(grads, heads_in[2].astype(f32), ((1,), (1,))) * decay[...]
    direct = mm_high(score_grad, heads_in[1].astype(f32), ((1,), (0,)))
    carried = mm_high(grads, incoming[...], ((1,), (1,)))
    q_grad[...] = (direct + grow[...] * carried).astype(bf16)
    k_part[...] = mm_high(score_grad, heads_in[0].astype(f32), ((0,), (0,)))
    v_part[...] = mm_high(scores[...], grads, ((0,), (0,)))


def last_kernel(place, heads_in, arrived, tails, keep, k_part, v_part, k_grad, v_grad):
    me = place[0]
    blocks, dh, _ = arrived.shape
    total = jnp.zeros((dh, dh), f32)
    gap = jnp.zeros((1, dh), f32)
    for block in range(blocks):
        weight = jnp.where(block > me, jnp.exp(gap), 0.0)
        total = total + weight * arrived[block].astype(f32)
        last = jnp.sum(tails[block, dh:, :].astype(f32), axis=0, keepdims=True)
        gap = gap + jnp.where(block > me, last, 0.0)
    from_values = mm_high(heads_in[2].astype(f32), total, ((1,), (1,)))
    from_keys = mm_high(heads_in[1].astype(f32), total, ((1,), (0,)))
    k_grad[...] = (k_part[...] + keep[...] * from_values).astype(bf16)
    v_grad[...] = (v_part[...] + keep[...] * from_keys).astype(bf16)


def local(
    resid, queries, keys, values, log_decay, w_out, w_up, w_down, expert_ids, route_weights, cotangent
):
    n_ctx, n_exp = lax.axis_size("ctx"), lax.axis_size("exp")
    chips = n_exp // 2
    place = jnp.stack([lax.axis_index("ctx"), lax.axis_index("exp")]).astype(jnp.int32)
    tokens, dh = queries.shape
    width = w_out.shape[1]
    share = width // n_exp
    cap = 4 * tokens // n_exp
    partner = [(i, i ^ 1) for i in range(n_exp)]
    same_core = [[2 * z + c for z in range(chips)] for c in range(2)]
    side = math.isqrt(n_ctx)
    axes = ("ctx", "exp")
    first, second = [], []
    for e in range(n_exp):
        along_y = [[(x * side + y) * n_exp + e for y in range(side)] for x in range(side)]
        along_x = [[(x * side + y) * n_exp + e for x in range(side)] for y in range(side)]
        first += along_x if e % 2 else along_y
        second += along_y if e % 2 else along_x
    square = (tokens, dh)
    flat = (share, tokens)
    weights, cot = route_weights.T, cotangent.T
    heads_in = jnp.stack([queries, keys, values])
    packed_rows = (n_exp, cap * 2 * share // 128, 128)

    [packed] = run_kernel(
        state_kernel,
        [((n_ctx, dh + ROWS, dh), bf16)],
        (keys, values, log_decay),
        far=3,
        scratch=[pltpu.VMEM(square, bf16)] * 2
        + [pltpu.VMEM(log_decay.shape, f32), pltpu.SemaphoreType.DMA((3,))],
        limit=56,
    )
    arrived = lax.all_to_all(packed, "ctx", 0, 0)
    scores, inner, decay, grow, keep, grown, w_mine, w_theirs = run_kernel(
        inner_kernel,
        [((tokens, tokens), f32), (square, f32), ((tokens, tokens), f32), (square, f32), (square, f32)]
        + [(square, f32)]
        + [((chips, share, dh), bf16)] * 2,
        (place, log_decay, w_out, heads_in),
        smem=1,
        raw=2,
    )
    w_given = lax.ppermute(w_theirs, "exp", partner)
    picks, cot_parts = run_kernel(
        functools.partial(route_kernel, cap=cap),
        [((n_exp * cap, 2 * tokens), bf16), ((share, 2 * tokens), bf16)],
        (expert_ids.T, weights, cot),
        raw=3,
    )
    heads, incoming = run_kernel(
        heads_kernel,
        [((tokens, dh), bf16), ((dh, dh), f32)],
        (place, arrived, inner, grown),
        smem=1,
    )
    heads_given = lax.ppermute(heads, "exp", partner)
    [pair] = run_kernel(
        project_kernel,
        [((chips, share, tokens), bf16)],
        (heads, heads_given, w_mine, w_given),
    )
    pieces = lax.all_to_all(pair, "exp", 0, 0, axis_index_groups=same_core)
    residual, sent = run_kernel(
        send_kernel,
        [(flat, bf16), (packed_rows, bf16)],
        (resid.T, pieces, cot_parts, picks),
        raw=1,
    )
    rows = lax.all_to_all(sent, "exp", 0, 0)
    packed, own, rstd = run_kernel(
        norm_kernel,
        [((side, 2 * cap, width), bf16), ((cap, width), bf16), ((cap, 128), f32)],
        (rows,),
    )
    line = lax.all_to_all(packed, axes, 0, 0, axis_index_groups=first)
    line = jnp.broadcast_to(line.reshape(1, side * 2 * cap, width), (side, side * 2 * cap, width))
    everyone = lax.all_to_all(line, axes, 0, 0, axis_index_groups=second)
    everyone = everyone.reshape(n_ctx, 2 * cap, width)
    [sums] = run_kernel(
        functools.partial(expert_kernel, step=1024 if width % 1024 == 0 else 384),
        [((n_ctx, 2 * cap, width), bf16)],
        (w_up[0], w_down[0], everyone),
        flops=2_400_000_000,
        moved=11_000_000,
    )
    sums = sums.reshape(side, side * 2 * cap, width)
    sums = lax.all_to_all(sums, axes, 0, 0, axis_index_groups=second)
    [sums] = run_kernel(
        functools.partial(half_kernel, step=128), [((side, 2 * cap, width), bf16)], (sums,)
    )
    sums = lax.all_to_all(sums, axes, 0, 0, axis_index_groups=first)
    [returned] = run_kernel(back_kernel, [(packed_rows, bf16)], (sums, own, rstd))
    returned = lax.all_to_all(returned, "exp", 0, 0)
    layer_out, resid_grad = run_kernel(
        join_kernel,
        [(flat, bf16), (flat, bf16)],
        (returned, picks, weights, residual, cot),
    )
    turned_grads = lax.all_gather(resid_grad, "exp", tiled=True)
    grad_heads, packed = run_kernel(
        state_grad_kernel,
        [(square, f32), ((n_ctx, dh, dh), bf16)],
        (w_out, turned_grads, grown),
    )
    states = lax.all_to_all(packed, "ctx", 0, 0)
    q_grad, k_part, v_part = run_kernel(
        grads_kernel,
        [(square, bf16), (square, f32), (square, f32)],
        (heads_in, grad_heads, scores, decay, grow, incoming),
    )
    k_grad, v_grad = run_kernel(
        last_kernel,
        [(square, bf16), (square, bf16)],
        (place, heads_in, states, arrived, keep, k_part, v_part),
        smem=1,
    )
    return layer_out.T, resid_grad.T, q_grad, k_grad, v_grad


def solution(mesh):
    both = P("ctx", "exp")
    rows = P("ctx", None)
    return jax.shard_map(
        local,
        mesh=mesh,
        in_specs=(
            both, both, both, both, P("exp", "ctx"), P("exp", None),
            P("exp", None, "ctx"), P("exp", "ctx", None), rows, rows, both,
        ),
        out_specs=(both,) * 5,
        check_vma=False,
    )
```

```python
import functools
import math

import jax
import jax.numpy as jnp
from jax import lax
from jax.experimental import pallas as pl
from jax.experimental.pallas import tpu as pltpu
from jax.sharding import PartitionSpec as P

bf16 = jnp.bfloat16
f32 = jnp.float32
ROWS = 16


def mm(a, b, dims):
    return lax.dot_general(a, b, (dims, ((), ())), preferred_element_type=f32)


def mm_high(a, b, dims):
    return lax.dot_general(
        a, b, (dims, ((), ())), precision=lax.Precision.HIGHEST, preferred_element_type=f32
    )


def iota(shape, axis):
    return lax.broadcasted_iota(jnp.int32, shape, axis)


def turned(column):
    n = column.shape[0]
    return jnp.sum(jnp.where(iota((n, n), 0) == iota((n, n), 1), column, 0.0), axis=0, keepdims=True)


def run_kernel(
    body, outs, args, smem=0, raw=0, far=0, scratch=(), flops=10_000_000, moved=1_000_000, limit=24
):
    vmem = pl.BlockSpec(memory_space=pltpu.VMEM)
    scalars = [pl.BlockSpec(memory_space=pltpu.SMEM)] * smem
    hbm = pl.BlockSpec(memory_space=pltpu.HBM)
    near = len(args) - smem - far - raw
    specs = scalars + [hbm] * far + [pl.BlockSpec()] * raw + [vmem] * near
    return pl.pallas_call(
        body,
        out_shape=[jax.ShapeDtypeStruct(shape, dtype) for shape, dtype in outs],
        in_specs=specs,
        out_specs=[vmem] * len(outs),
        scratch_shapes=scratch,
        compiler_params=pltpu.CompilerParams(vmem_limit_bytes=limit << 20),
        cost_estimate=pl.CostEstimate(flops=flops, bytes_accessed=moved, transcendentals=0),
    )(*args)


def pack(left, right):
    both = jnp.concatenate([left, right], axis=2)
    lanes, half = 128, both.shape[1] // 2
    rest = both[:, :, lanes:]
    rest = jnp.concatenate([rest[:, :half], rest[:, half:]], axis=2)
    return jnp.concatenate([both[:, :, :lanes], rest], axis=1)


def unpack(rows, share):
    lanes, half = 128, rows.shape[1] // 3
    top, low = rows[:, : 2 * half], rows[:, 2 * half :]
    rest = lanes // 2
    low = jnp.concatenate([low[:, :, :rest], low[:, :, rest:]], axis=1)
    both = jnp.concatenate([top, low], axis=2)
    return both[:, :, :share], both[:, :, share:]


def running(decay_row):
    n = decay_row.shape[1]
    causal = iota((n, n), 0) >= iota((n, n), 1)
    return jnp.sum(jnp.where(causal, decay_row, 0.0), axis=1, keepdims=True)


def state_kernel(keys_far, values_far, decay_far, packed, keys, values, log_decay, arrivals):
    pairs = ((keys_far, keys), (values_far, values), (decay_far, log_decay))
    copies = [pltpu.make_async_copy(a, b, arrivals.at[i]) for i, (a, b) in enumerate(pairs)]
    for copy in copies:
        copy.start()
    for copy in copies:
        copy.wait()
    cum = running(log_decay[...])
    n = cum.shape[0]
    last = cum[n - 1 :, :]
    kept = keys[...].astype(f32) * jnp.exp(last - cum)
    state = mm_high(kept, values[...].astype(f32), ((0,), (0,))).astype(bf16)
    dh = state.shape[1]
    high = last.astype(bf16).astype(f32)
    mid = (last - high).astype(bf16).astype(f32)
    low = last - high - mid
    row = iota((ROWS, dh), 0)
    tail = jnp.where(row == 0, high, jnp.where(row == 1, mid, jnp.where(row == 2, low, 0.0)))
    for block in range(packed.shape[0]):
        packed[block, :dh, :] = state
        packed[block, dh:, :] = tail.astype(bf16)


def inner_kernel(
    place, log_decay, w_out, heads_in, scores, inner, decay, grow, keep, grown, mine, theirs
):
    cum = running(log_decay[...])
    n = cum.shape[0]
    causal = iota((n, n), 0) >= iota((n, n), 1)
    gaps = jnp.where(causal, cum - turned(cum), 0.0)
    fall = jnp.where(causal, jnp.exp(gaps), 0.0)
    pairs = mm_high(heads_in[0].astype(f32), heads_in[1].astype(f32), ((1,), (1,))) * fall
    scores[...] = pairs
    decay[...] = fall
    inner[...] = mm_high(pairs, heads_in[2].astype(f32), ((1,), (0,)))
    grow[...] = jnp.broadcast_to(jnp.exp(cum), grow.shape)
    grown[...] = heads_in[0].astype(f32) * jnp.exp(cum)
    keep[...] = jnp.broadcast_to(jnp.exp(cum[n - 1 :, :] - cum), keep.shape)
    dh, width = w_out.shape
    chips, share, _ = mine.shape
    blocks = [w_out[:, at : at + dh].astype(f32).T.astype(bf16) for at in range(0, width, dh)]
    flipped = jnp.concatenate(blocks, axis=0).reshape(chips, 2, share, dh)
    even = lax.rem(place[1], 2) == 0
    mine[...] = jnp.where(even, flipped[:, 0], flipped[:, 1])
    theirs[...] = jnp.where(even, flipped[:, 1], flipped[:, 0])


def route_kernel(ids, weights, cotangent, picks, cot_parts, *, cap):
    _, tokens = ids.shape
    slots_all = picks.shape[0]
    experts = slots_all // cap
    chosen = [(ids[j : j + 1, :] == iota((experts, tokens), 0)).astype(f32) for j in range(2)]
    earlier = (iota((tokens, tokens), 0) < iota((tokens, tokens), 1)).astype(f32).astype(bf16)
    before = mm((chosen[0] + chosen[1]).astype(bf16), earlier, ((1,), (0,)))
    cot = cotangent[...].astype(f32)
    for j in range(2):
        slot = jnp.sum(before * chosen[j], axis=0, keepdims=True)
        position = ids[j : j + 1, :].astype(f32) * cap + slot
        down = iota((slots_all, tokens), 0).astype(f32)
        at = slice(j * tokens, (j + 1) * tokens)
        picks[:, at] = (position == down).astype(f32).astype(bf16)
        cot_parts[:, at] = (weights[j : j + 1, :] * cot).astype(bf16)


def heads_kernel(place, arrived, inner, grown, heads, incoming):
    me = place[0]
    blocks = arrived.shape[0]
    dh = grown.shape[1]
    total = jnp.zeros((dh, dh), f32)
    gap = jnp.zeros((1, dh), f32)
    for block in reversed(range(blocks)):
        weight = jnp.where(block < me, jnp.exp(gap), 0.0)
        total = total + weight * arrived[block, :dh, :].astype(f32)
        last = jnp.sum(arrived[block, dh:, :].astype(f32), axis=0, keepdims=True)
        gap = gap + jnp.where(block < me, last, 0.0)
    incoming[...] = total
    heads[...] = (inner[...] + mm_high(grown[...], total, ((1,), (0,)))).astype(bf16)


def project_kernel(heads, heads_given, weights, weights_given, picks, partial):
    del picks
    chips, share, dh = weights.shape
    both = jnp.concatenate([weights[...], weights_given[...]], axis=2).reshape(chips * share, 2 * dh)
    pair = jnp.concatenate([heads[...], heads_given[...]], axis=1)
    partial[...] = mm(both, pair, ((1,), (1,))).astype(bf16).reshape(partial.shape)


def send_kernel(resid, pieces, cot_parts, picks, residual, sent):
    attn = jnp.sum(pieces[...].astype(f32), axis=0).astype(bf16).astype(f32)
    total = (resid[...].astype(f32) + attn).astype(bf16)
    residual[...] = total
    tokens = total.shape[1]
    placed = picks[:, :tokens] + picks[:, tokens:]
    share = total.shape[0]
    experts, rows_each, _ = sent.shape
    cap = picks.shape[0] // experts
    rows = mm(placed, total, ((1,), (1,))).reshape(experts, cap, share)
    grads = mm(picks[...], cot_parts[...], ((1,), (1,))).reshape(experts, cap, share)
    sent[...] = pack(rows, grads).astype(bf16)


def norm_kernel(rows, packed, own, rstd_out):
    experts = rows.shape[0]
    blocks, both, width = packed.shape
    cap, share = both // 2, width // experts
    left, right = unpack(rows[...].astype(f32), share)
    whole = jnp.concatenate([left[e] for e in range(experts)], axis=1)
    grads = jnp.concatenate([right[e] for e in range(experts)], axis=1).astype(bf16)
    rstd = lax.rsqrt(jnp.sum(whole * whole, axis=1, keepdims=True) / width + 1e-6)
    own[...] = whole.astype(bf16)
    rstd_out[...] = jnp.broadcast_to(rstd, rstd_out.shape)
    normed = (whole * rstd).astype(bf16)
    for block in range(blocks):
        packed[block, :cap, :] = normed
        packed[block, cap:, :] = grads


def expert_kernel(w_up, w_down, everyone, sums, *, step):
    blocks, both, width = everyone.shape
    cap = both // 2
    rows = blocks * cap
    hidden = w_up.shape[1]
    upper = jnp.zeros((rows, hidden), f32)
    grad_act = jnp.zeros((rows, hidden), f32)
    for start in range(0, width, step):
        at = slice(start, start + step)
        x = everyone[:, :cap, at].reshape(rows, step)
        g = everyone[:, cap:, at].reshape(rows, step)
        upper = upper + mm(x, w_up[at, :], ((1,), (0,)))
        grad_act = grad_act + mm(g, w_down[:, at], ((1,), (1,)))
    sigma = 1.0 / (1.0 + jnp.exp(-upper))
    act = (upper * sigma).astype(bf16)
    grad_up = (grad_act * (sigma * (1.0 + upper * (1.0 - sigma)))).astype(bf16)
    for start in range(0, width, step):
        at = slice(start, start + step)
        out = mm(act, w_down[:, at], ((1,), (0,))).astype(bf16)
        back = mm(grad_up, w_up[at, :], ((1,), (1,))).astype(bf16)
        sums[:, :cap, at] = out.reshape(blocks, cap, step)
        sums[:, cap:, at] = back.reshape(blocks, cap, step)


def half_kernel(sums, out, *, step):
    for start in range(0, out.shape[2], step):
        at = slice(start, start + step)
        total = jnp.sum(sums[:, :, at].astype(f32), axis=0).astype(bf16)
        out[:, :, at] = total.reshape(out.shape[0], out.shape[1], step)


def back_kernel(sums, own, rstd_in, returned):
    experts = returned.shape[0]
    total = jnp.sum(sums[...].astype(f32), axis=0)
    cap, width = own.shape
    share = width // experts
    out, grads = total[:cap], total[cap:].astype(bf16).astype(f32)
    rows = own[...].astype(f32)
    rstd = rstd_in[:, :1]
    inner = jnp.sum(grads * rows, axis=1, keepdims=True)
    grads = rstd * grads - rows * (rstd * rstd * rstd * inner / width)
    left = jnp.stack([out[:, e * share : (e + 1) * share] for e in range(experts)])
    right = jnp.stack([grads[:, e * share : (e + 1) * share] for e in range(experts)])
    returned[...] = pack(right, left).astype(bf16)


def resid_grad_kernel(returned, picks, cotangent, resid_grad):
    share, tokens = cotangent.shape
    slots_all = picks.shape[0]
    rows = returned[:, : 2 * returned.shape[1] // 3, :share].reshape(slots_all, share)
    summed = mm(rows, picks[:, :tokens] + picks[:, tokens:], ((0,), (0,)))
    resid_grad[...] = (cotangent[...].astype(f32) + summed).astype(bf16)


def layer_out_kernel(returned, picks, weights, residual, layer_out):
    share, tokens = residual.shape
    slots_all = picks.shape[0]
    _, outs = unpack(returned[...].astype(f32), share)
    both = mm(outs.reshape(slots_all, share).astype(bf16), picks[...], ((0,), (0,)))
    routed = weights[0:1, :] * both[:, :tokens] + weights[1:2, :] * both[:, tokens:]
    layer_out[...] = (residual[...].astype(f32) + routed).astype(bf16)


def state_grad_kernel(w_out, turned_grads, grown, grad_heads, packed):
    flipped = mm(w_out[...], turned_grads[...], ((1,), (0,)))
    grads = flipped.T
    grad_heads[...] = grads
    state = mm_high(grown[...], grads, ((0,), (0,))).astype(bf16)
    for block in range(packed.shape[0]):
        packed[block] = state


def grads_kernel(
    heads_in, grad_heads, scores, decay, grow, incoming, q_grad, k_part, v_part
):
    grads = grad_heads[...]
    score_grad = mm_high(grads, heads_in[2].astype(f32), ((1,), (1,))) * decay[...]
    direct = mm_high(score_grad, heads_in[1].astype(f32), ((1,), (0,)))
    carried = mm_high(grads, incoming[...], ((1,), (1,)))
    q_grad[...] = (direct + grow[...] * carried).astype(bf16)
    k_part[...] = mm_high(score_grad, heads_in[0].astype(f32), ((0,), (0,)))
    v_part[...] = mm_high(scores[...], grads, ((0,), (0,)))


def last_kernel(place, heads_in, arrived, tails, keep, k_part, v_part, k_grad, v_grad):
    me = place[0]
    blocks, dh, _ = arrived.shape
    total = jnp.zeros((dh, dh), f32)
    gap = jnp.zeros((1, dh), f32)
    for block in range(blocks):
        weight = jnp.where(block > me, jnp.exp(gap), 0.0)
        total = total + weight * arrived[block].astype(f32)
        last = jnp.sum(tails[block, dh:, :].astype(f32), axis=0, keepdims=True)
        gap = gap + jnp.where(block > me, last, 0.0)
    from_values = mm_high(heads_in[2].astype(f32), total, ((1,), (1,)))
    from_keys = mm_high(heads_in[1].astype(f32), total, ((1,), (0,)))
    k_grad[...] = (k_part[...] + keep[...] * from_values).astype(bf16)
    v_grad[...] = (v_part[...] + keep[...] * from_keys).astype(bf16)


def local(
    resid, queries, keys, values, log_decay, w_out, w_up, w_down, expert_ids, route_weights, cotangent
):
    n_ctx, n_exp = lax.axis_size("ctx"), lax.axis_size("exp")
    chips = n_exp // 2
    place = jnp.stack([lax.axis_index("ctx"), lax.axis_index("exp")]).astype(jnp.int32)
    tokens, dh = queries.shape
    width = w_out.shape[1]
    share = width // n_exp
    cap = 4 * tokens // n_exp
    partner = [(i, i ^ 1) for i in range(n_exp)]
    same_core = [[2 * z + c for z in range(chips)] for c in range(2)]
    side = math.isqrt(n_ctx)
    axes = ("ctx", "exp")
    first, second = [], []
    for e in range(n_exp):
        along_y = [[(x * side + y) * n_exp + e for y in range(side)] for x in range(side)]
        along_x = [[(x * side + y) * n_exp + e for x in range(side)] for y in range(side)]
        first += along_x if e % 2 else along_y
        second += along_y if e % 2 else along_x
    square = (tokens, dh)
    flat = (share, tokens)
    weights, cot = route_weights.T, cotangent.T
    heads_in = jnp.stack([queries, keys, values])
    packed_rows = (n_exp, cap * 2 * share // 128, 128)

    [packed] = run_kernel(
        state_kernel,
        [((n_ctx, dh + ROWS, dh), bf16)],
        (keys, values, log_decay),
        far=3,
        scratch=[pltpu.VMEM(square, bf16)] * 2
        + [pltpu.VMEM(log_decay.shape, f32), pltpu.SemaphoreType.DMA((3,))],
        limit=56,
    )
    arrived = lax.all_to_all(packed, "ctx", 0, 0)
    scores, inner, decay, grow, keep, grown, w_mine, w_theirs = run_kernel(
        inner_kernel,
        [((tokens, tokens), f32), (square, f32), ((tokens, tokens), f32), (square, f32), (square, f32)]
        + [(square, f32)]
        + [((chips, share, dh), bf16)] * 2,
        (place, log_decay, w_out, heads_in),
        smem=1,
        raw=2,
    )
    w_given = lax.ppermute(w_theirs, "exp", partner)
    picks, cot_parts = run_kernel(
        functools.partial(route_kernel, cap=cap),
        [((n_exp * cap, 2 * tokens), bf16), ((share, 2 * tokens), bf16)],
        (expert_ids.T, weights, cot),
        raw=3,
    )
    heads, incoming = run_kernel(
        heads_kernel,
        [((tokens, dh), bf16), ((dh, dh), f32)],
        (place, arrived, inner, grown),
        smem=1,
    )
    heads_given = lax.ppermute(heads, "exp", partner)
    [pair] = run_kernel(
        project_kernel,
        [((chips, share, tokens), bf16)],
        (heads, heads_given, w_mine, w_given, picks),
    )
    pieces = lax.all_to_all(pair, "exp", 0, 0, axis_index_groups=same_core)
    residual, sent = run_kernel(
        send_kernel,
        [(flat, bf16), (packed_rows, bf16)],
        (resid.T, pieces, cot_parts, picks),
        raw=1,
    )
    rows = lax.all_to_all(sent, "exp", 0, 0)
    packed, own, rstd = run_kernel(
        norm_kernel,
        [((side, 2 * cap, width), bf16), ((cap, width), bf16), ((cap, 128), f32)],
        (rows,),
    )
    line = lax.all_to_all(packed, axes, 0, 0, axis_index_groups=first)
    line = jnp.broadcast_to(line.reshape(1, side * 2 * cap, width), (side, side * 2 * cap, width))
    everyone = lax.all_to_all(line, axes, 0, 0, axis_index_groups=second)
    everyone = everyone.reshape(n_ctx, 2 * cap, width)
    [sums] = run_kernel(
        functools.partial(expert_kernel, step=1024 if width % 1024 == 0 else 384),
        [((n_ctx, 2 * cap, width), bf16)],
        (w_up[0], w_down[0], everyone),
        flops=2_400_000_000,
        moved=11_000_000,
    )
    sums = sums.reshape(side, side * 2 * cap, width)
    sums = lax.all_to_all(sums, axes, 0, 0, axis_index_groups=second)
    [sums] = run_kernel(
        functools.partial(half_kernel, step=128), [((side, 2 * cap, width), bf16)], (sums,)
    )
    sums = lax.all_to_all(sums, axes, 0, 0, axis_index_groups=first)
    [returned] = run_kernel(back_kernel, [(packed_rows, bf16)], (sums, own, rstd))
    returned = lax.all_to_all(returned, "exp", 0, 0)
    [resid_grad] = run_kernel(resid_grad_kernel, [(flat, bf16)], (returned, picks, cot))
    turned_grads = lax.all_gather(resid_grad, "exp", tiled=True)
    grad_heads, packed = run_kernel(
        state_grad_kernel,
        [(square, f32), ((n_ctx, dh, dh), bf16)],
        (w_out, turned_grads, grown),
    )
    states = lax.all_to_all(packed, "ctx", 0, 0)
    q_grad, k_part, v_part = run_kernel(
        grads_kernel,
        [(square, bf16), (square, f32), (square, f32)],
        (heads_in, grad_heads, scores, decay, grow, incoming),
    )
    [layer_out] = run_kernel(
        layer_out_kernel, [(flat, bf16)], (returned, picks, weights, residual)
    )
    k_grad, v_grad = run_kernel(
        last_kernel,
        [(square, bf16), (square, bf16)],
        (place, heads_in, states, arrived, keep, k_part, v_part),
        smem=1,
    )
    return layer_out.T, resid_grad.T, q_grad, k_grad, v_grad


def solution(mesh):
    both = P("ctx", "exp")
    rows = P("ctx", None)
    return jax.shard_map(
        local,
        mesh=mesh,
        in_specs=(
            both, both, both, both, P("exp", "ctx"), P("exp", None),
            P("exp", None, "ctx"), P("exp", "ctx", None), rows, rows, both,
        ),
        out_specs=(both,) * 5,
        check_vma=False,
    )
```
